1024 devices in a mesh: dp: 64 (over z, y_lo, core), tensor: 16 (over y_hi, x).
Axes of the slice: x: 8, y: 8 (y_hi: 2, y_lo: 4; y = y_hi * 4 + y_lo), z: 8, core: 2. Of those that a mesh axis runs over, the one named last changes fastest.
Arguments:
- policy: bfloat16 [64, 128, 16384], P('dp', 'tensor'), may hold values from -4 to 4
- ref_weight: bfloat16 [8192, 16384], P('tensor', 'dp'), may hold values from -4 to 4
- tokens: bfloat16 [2, 3072, 8192], P(None, 'dp', 'tensor'), may hold values from -400 to 400
- gain: float32 [8192], P('tensor'), may hold values from 0.5 to 2
Outputs:
- blended: bfloat16 [8192, 16384], P('tensor', 'dp')
- activated: bfloat16 [2, 3072, 16384], P(None, 'tensor', 'dp')
The draws below stay inside these ranges and needn't reach their ends.
All inputs are finite; a program needn't handle non-finite values.
Results may differ from the reference program's by a relative error of at most 0.022.
Values may be sent and summed in bfloat16 or wider, within the bound.
No kernel may reach another device: no remote copies, remote signals or barrier semaphores. Data moves between devices by JAX's collectives and lax.ppermute only.
A program may use at most 64 MiB of HBM per device.

```python
import math
import jax
import jax.numpy as jnp
from jax import lax

D = 8192
FF = 16384
MICRO = 2
TOKENS = 3072
N_DP = 64
N_TENSOR = 16


def draw_tokens(key, part):
    key = jax.random.fold_in(key, 11)
    key_val, key_row, key_col = jax.random.split(key, 3)
    values = jnp.clip(jax.random.normal(key_val, (MICRO, TOKENS, D), jnp.float32), -4.0, 4.0)
    row_scale = 10.0 ** jax.random.uniform(key_row, (MICRO, TOKENS, 1), jnp.float32)
    ramp = jnp.arange(D, dtype=jnp.float32) / D
    col_scale = 10.0 ** (0.5 * ramp + 0.5 * jax.random.uniform(key_col, (D,), jnp.float32))
    return (values * row_scale * col_scale).astype(jnp.bfloat16)


def shard_levels(stream_key, shape, cuts, low, largest):
    factor_of = 1.0
    for position, shards_of in cuts:
        heights = jax.random.uniform(jax.random.fold_in(jax.random.fold_in(stream_key, 6), position), (shards_of,), jnp.float32, low / len(cuts), largest / len(cuts))
        factor_of = factor_of * jnp.repeat(jnp.exp(heights), shape[position] // shards_of).reshape((-1,) + (1,) * (len(shape) - 1 - position))
    return factor_of


def gaussian(rng, extent, scale, most, shards=(), kind=jnp.bfloat16):
    values = scale * jax.random.normal(rng, extent, jnp.float32)
    if shards:
        values = values * shard_levels(rng, extent, shards, -0.22, 0.18)
    return jnp.clip(values, -most, most).astype(kind)


def setup_inputs(seed: int = 0) -> dict:
    key_of = jax.random.split(jax.random.key(seed), 5)
    policy = gaussian(key_of[0], (N_DP, D // N_DP, FF), 1.0, 4.0, ((0, 64), (1, 16)))
    ref_weight = gaussian(key_of[1], (D, FF), 1.0, 4.0, ((0, 16), (1, 64)))
    tokens = draw_tokens(jax.random.fold_in(key_of[4], 71), 0)
    gain = jnp.clip(jnp.exp(math.log(2.0) - 1.3862944 * jax.random.uniform(key_of[3], (D,), jnp.float32) ** shard_levels(key_of[3], (D,), ((0, 16),), -0.2, 0.2)), 0.5, 2.0)
    return dict(policy=policy, ref_weight=ref_weight, tokens=tokens, gain=gain)


ema_rate = 0.5
norm_eps = 1e-06

def reference(policy, ref_weight, tokens, gain):
    shard_rows = D // (N_DP * N_TENSOR)
    policy_matrix = policy.reshape(N_DP, N_TENSOR, shard_rows, FF).transpose(1, 0, 2, 3).reshape(D, FF)
    ref_f = ref_weight.astype(jnp.float32)
    blended = (ref_f + ema_rate * (policy_matrix.astype(jnp.float32) - ref_f)).astype(jnp.bfloat16)
    tok_f = tokens.astype(jnp.float32)
    squares = lax.optimization_barrier(jnp.sum(tok_f * tok_f, axis=2, keepdims=True))
    normed = (tok_f * lax.rsqrt(squares / D + norm_eps) * gain).astype(jnp.bfloat16)
    normed = normed.reshape(MICRO * TOKENS, D)
    local_width = D // N_TENSOR
    out_scale = 1.0 / math.sqrt(D)

    def add_block(index, summed):
        offset = (index * local_width).astype(jnp.int32)
        columns = lax.dynamic_slice_in_dim(normed, offset, local_width, 1)
        weights = lax.dynamic_slice_in_dim(blended, offset, local_width, 0)
        partial_term = jnp.dot(columns, weights, preferred_element_type=jnp.float32) * out_scale
        rounded = lax.optimization_barrier(partial_term.astype(jnp.bfloat16))
        return summed + rounded.astype(jnp.float32)
    summed = lax.fori_loop(0, N_TENSOR, add_block, jnp.zeros((MICRO * TOKENS, FF), jnp.float32))
    activated = jax.nn.silu(summed).astype(jnp.bfloat16).reshape(MICRO, TOKENS, FF)
    return (blended, activated)
```

```python
import math

import jax
import jax.numpy as jnp
from jax import lax
from jax.experimental import pallas as pl
from jax.experimental.pallas import tpu as pltpu
from jax.sharding import Mesh
from jax.sharding import PartitionSpec as P

D = 8192
AXES = ("z", "yl", "c", "yh", "x")
NZ, NYL, NC, NYH, NX = SIZES = (8, 4, 2, 2, 8)

ema_rate = 0.5
norm_eps = 1e-06


def flat(z, yl, c, yh, x):
    return (((z * NYL + yl) * NC + c) * NYH + yh) * NX + x


def token_moves(e):
    moves = []
    for j in range(NZ * NYL * NC):
        i, a = divmod(j, 4)
        yh2, x = divmod(i, NX)
        z, rest = divmod(j, NYL * NC)
        yl, c = divmod(rest, NC)
        for yh in range(NYH):
            for x2 in range(NX):
                to = flat(x2, (2 * yh2 + a // 2) ^ e, a % 2, yh, x)
                moves.append((flat(z, yl, c, yh, x2), to))
    return moves


def shift(count, by):
    return [(i, (i + by) % count) for i in range(count)]


def core_shift():
    moves = []
    for z in range(NZ):
        for c in range(NC):
            to = (z + (1 if c == 0 else -1)) % NZ
            moves.append((z * NC + c, to * NC + c))
    return moves


def gate_kernel(place, rows_of, *refs):
    blocks, weights = refs[:NX], refs[NX : 2 * NX]
    kept, sent, a_buf, b_buf, acc, a_sem, b_sem = refs[2 * NX :]
    b_copies = [
        pltpu.make_async_copy(w, b_buf.at[place[d]], b_sem.at[d]) for d, w in enumerate(weights)
    ]
    a_copies = [
        pltpu.make_async_copy(b, a_buf.at[s], a_sem.at[s]) for s, b in enumerate(blocks)
    ]
    for copy in b_copies + a_copies:
        copy.start()
    for copy in b_copies:
        copy.wait()
    for s, copy in enumerate(a_copies):
        copy.wait()
        part = jnp.dot(a_buf[s], b_buf[s], preferred_element_type=jnp.float32)
        acc[...] = part if s == 0 else acc[...] + part
    size = kept.shape[0] // 4
    for b in range(2):
        for core in range(NC):
            to = pl.ds((b * NC + core) * size, size)
            mine = pl.multiple_of((core * NYL + rows_of[b]) * size, size)
            theirs = pl.multiple_of((core * NYL + rows_of[2 + b]) * size, size)
            kept[to, :] = acc[pl.ds(mine, size), :]
            sent[to, :] = acc[pl.ds(theirs, size), :].astype(sent.dtype)


def gate_parts(place, rows_of, blocks, weights):
    rows, depth = blocks[0].shape
    cols = weights[0].shape[1]
    smem = pl.BlockSpec(memory_space=pltpu.SMEM)
    hbm = pl.BlockSpec(memory_space=pl.ANY)
    vmem = pl.BlockSpec(memory_space=pltpu.VMEM)
    half = rows // 2
    return pl.pallas_call(
        gate_kernel,
        out_shape=(
            jax.ShapeDtypeStruct((half, cols), jnp.float32),
            jax.ShapeDtypeStruct((half, cols), jnp.bfloat16),
        ),
        in_specs=[smem, smem] + [hbm] * (2 * NX),
        out_specs=(vmem, vmem),
        scratch_shapes=[
            pltpu.VMEM((NX, rows, depth), jnp.bfloat16),
            pltpu.VMEM((NX, depth, cols), jnp.bfloat16),
            pltpu.VMEM((rows, cols), jnp.float32),
            pltpu.SemaphoreType.DMA((NX,)),
            pltpu.SemaphoreType.DMA((NX,)),
        ],
        compiler_params=pltpu.CompilerParams(vmem_limit_bytes=48 * 2**20),
        cost_estimate=pl.CostEstimate(
            flops=2 * NX * rows * depth * cols,
            bytes_accessed=2 * NX * depth * (rows + cols),
            transcendentals=0,
        ),
    )(place, rows_of, *blocks, *weights)


def body(policy, ref_weight, tokens, gain):
    z, yl, c, yh, x = (lax.axis_index(a) for a in AXES)
    micro, toks, width = tokens.shape
    pieces = policy.reshape(8, NZ * NYL * NC, 256).transpose(1, 0, 2)
    arrived = lax.all_to_all(pieces, ("z", "yl", "c"), 0, 0, tiled=True)
    four = jnp.stack([lax.ppermute(tokens, AXES, token_moves(e)) for e in range(NYL)])
    four = four.reshape(NYL * micro * toks, width)
    four, arrived = lax.optimization_barrier((four, arrived))
    other = lax.ppermute(four, "c", shift(NC, 1))
    first = c == 0
    own = jnp.concatenate([jnp.where(first, four, other), jnp.where(first, other, four)])
    policy_slice = arrived.reshape(ref_weight.shape)
    ref_f = ref_weight.astype(jnp.float32)
    blended = (ref_f + ema_rate * (policy_slice.astype(jnp.float32) - ref_f)).astype(jnp.bfloat16)
    scaled = (blended.astype(jnp.float32) * gain[:, None]).astype(jnp.bfloat16)
    sign = 1 - 2 * c
    blocks, weights = [own] + [None] * (NX - 1), [scaled] + [None] * (NX - 1)
    travelling, up, down = own, scaled, scaled
    half = NX // 2
    for step in range(1, half + 1):
        if step > 1:
            travelling, up, down = lax.optimization_barrier((travelling, up, down))
        arriving = lax.ppermute(travelling, ("z", "c"), core_shift())
        up = lax.ppermute(up, "x", shift(NX, 1))
        if step < half:
            down = lax.ppermute(down, "x", shift(NX, -1))
        if step > 1:
            blocks[step - 1] = lax.ppermute(travelling, "c", shift(NC, 1))
        travelling = arriving
        blocks[NX - step], weights[NX - step] = travelling, up
        if step < half:
            weights[step] = down
    squares = 0.0
    for block in blocks:
        block_f = block.astype(jnp.float32)
        squares = squares + jnp.sum(block_f * block_f, axis=1)
    squares = squares.reshape(NC, NYL, 1, micro * toks)

    def rows_of(group):
        return [yl ^ (2 * group + b) for b in range(2)]

    def part(v, group):
        return jnp.stack(
            [lax.dynamic_index_in_dim(v, q, 1, keepdims=False) for q in rows_of(group)]
        ).reshape(1, -1)

    swap = shift(NYH, 1)
    squares = part(squares, yh) + lax.ppermute(part(squares, 1 - yh), "yh", swap)
    place = jnp.stack([(sign * (x + d - z)) % NX for d in range(NX)])
    kept, sent = gate_parts(
        place, jnp.stack(rows_of(yh) + rows_of(1 - yh)), blocks, weights
    )
    other = lax.ppermute(sent, "yh", swap)
    factor = lax.rsqrt(squares.reshape(-1, 1) / D + norm_eps) * (1.0 / math.sqrt(D))
    gate = (kept + other.astype(jnp.float32)) * factor
    activated = jax.nn.silu(gate).astype(jnp.bfloat16)
    activated = activated.reshape(4, micro, toks, -1).transpose(1, 0, 2, 3)
    return blended, activated.reshape(micro, 4 * toks, -1)


def solution(mesh):
    fine = Mesh(mesh.devices.reshape(SIZES), AXES)
    dp, tensor = ("z", "yl", "c"), ("yh", "x")
    return jax.shard_map(
        body,
        mesh=fine,
        in_specs=(P(dp, tensor, None), P(tensor, dp), P(None, dp, tensor), P(tensor)),
        out_specs=(P(tensor, dp), P(None, tensor, dp)),
        check_vma=False,
    )
```

```python
import math

import jax
import jax.numpy as jnp
from jax import lax
from jax.experimental import pallas as pl
from jax.experimental.pallas import tpu as pltpu
from jax.sharding import Mesh
from jax.sharding import PartitionSpec as P

D = 8192
AXES = ("z", "yl", "c", "yh", "x")
NZ, NYL, NC, NYH, NX = SIZES = (8, 4, 2, 2, 8)

ema_rate = 0.5
norm_eps = 1e-06


def flat(z, yl, c, yh, x):
    return (((z * NYL + yl) * NC + c) * NYH + yh) * NX + x


def token_moves():
    moves = []
    for j in range(NZ * NYL * NC):
        i, a = divmod(j, 4)
        yh2, x = divmod(i, NX)
        z, rest = divmod(j, NYL * NC)
        yl, c = divmod(rest, NC)
        for yh in range(NYH):
            for x2 in range(NX):
                to = flat(x2, 2 * yh2 + a // 2, a % 2, yh, x)
                moves.append((flat(z, yl, c, yh, x2), to))
    return moves


def shift(count, by):
    return [(i, (i + by) % count) for i in range(count)]


def core_shift():
    moves = []
    for z in range(NZ):
        for c in range(NC):
            to = (z + (1 if c == 0 else -1)) % NZ
            moves.append((z * NC + c, to * NC + c))
    return moves


def gate_kernel(place, rows_of, *refs):
    blocks, weights = refs[:NX], refs[NX]
    kept, sent, a_buf, b_buf, acc, a_sem, b_sem = refs[NX + 1 :]
    b_copies = [
        pltpu.make_async_copy(weights.at[d], b_buf.at[place[d]], b_sem.at[d]) for d in range(NX)
    ]
    a_copies = [
        pltpu.make_async_copy(b, a_buf.at[s], a_sem.at[s]) for s, b in enumerate(blocks)
    ]
    for copy in b_copies + a_copies:
        copy.start()
    for copy in b_copies:
        copy.wait()
    for s, copy in enumerate(a_copies):
        copy.wait()
        part = jnp.dot(a_buf[s], b_buf[s], preferred_element_type=jnp.float32)
        acc[...] = part if s == 0 else acc[...] + part
    size = kept.shape[0] // 4
    for b in range(2):
        for core in range(NC):
            to = pl.ds((b * NC + core) * size, size)
            mine = pl.multiple_of((core * NYL + rows_of[b]) * size, size)
            theirs = pl.multiple_of((core * NYL + rows_of[2 + b]) * size, size)
            kept[to, :] = acc[pl.ds(mine, size), :]
            sent[to, :] = acc[pl.ds(theirs, size), :].astype(sent.dtype)


def gate_parts(place, rows_of, blocks, weights):
    rows, depth = blocks[0].shape
    cols = weights.shape[2]
    smem = pl.BlockSpec(memory_space=pltpu.SMEM)
    hbm = pl.BlockSpec(memory_space=pl.ANY)
    vmem = pl.BlockSpec(memory_space=pltpu.VMEM)
    half = rows // 2
    return pl.pallas_call(
        gate_kernel,
        out_shape=(
            jax.ShapeDtypeStruct((half, cols), jnp.float32),
            jax.ShapeDtypeStruct((half, cols), jnp.bfloat16),
        ),
        in_specs=[smem, smem] + [hbm] * (NX + 1),
        out_specs=(vmem, vmem),
        scratch_shapes=[
            pltpu.VMEM((NX, rows, depth), jnp.bfloat16),
            pltpu.VMEM((NX, depth, cols), jnp.bfloat16),
            pltpu.VMEM((rows, cols), jnp.float32),
            pltpu.SemaphoreType.DMA((NX,)),
            pltpu.SemaphoreType.DMA((NX,)),
        ],
        compiler_params=pltpu.CompilerParams(vmem_limit_bytes=48 * 2**20),
        cost_estimate=pl.CostEstimate(
            flops=2 * NX * rows * depth * cols,
            bytes_accessed=2 * NX * depth * (rows + cols),
            transcendentals=0,
        ),
    )(place, rows_of, *blocks, weights)


def body(policy, ref_weight, tokens, gain):
    z, yl, c, yh, x = (lax.axis_index(a) for a in AXES)
    micro, toks, width = tokens.shape
    pieces = policy.reshape(8, NZ * NYL * NC, 256).transpose(1, 0, 2)
    arrived = lax.all_to_all(pieces, ("z", "yl", "c"), 0, 0, tiled=True)
    moved = lax.ppermute(tokens, AXES, token_moves())
    four = jnp.stack(
        [moved] + [lax.ppermute(moved, "yl", [(i, i ^ e) for i in range(NYL)]) for e in range(1, NYL)]
    )
    four = four.reshape(NYL * micro * toks, width)
    four, arrived = lax.optimization_barrier((four, arrived))
    other = lax.ppermute(four, "c", shift(NC, 1))
    first = c == 0
    own = jnp.concatenate([jnp.where(first, four, other), jnp.where(first, other, four)])
    policy_slice = arrived.reshape(ref_weight.shape)
    ref_f = ref_weight.astype(jnp.float32)
    blended = (ref_f + ema_rate * (policy_slice.astype(jnp.float32) - ref_f)).astype(jnp.bfloat16)
    scaled = (blended.astype(jnp.float32) * gain[:, None]).astype(jnp.bfloat16)
    weights = lax.all_to_all(
        jnp.broadcast_to(scaled[None], (NX,) + scaled.shape), "x", 0, 0, tiled=True
    )
    sign = 1 - 2 * c
    blocks, travelling = [own] + [None] * (NX - 1), own
    half = NX // 2
    for step in range(1, half + 1):
        travelling = lax.ppermute(travelling, ("z", "c"), core_shift())
        blocks[NX - step] = travelling
        if step < half:
            blocks[step] = lax.ppermute(travelling, "c", shift(NC, 1))
    squares = 0.0
    for block in blocks:
        block_f = block.astype(jnp.float32)
        squares = squares + jnp.sum(block_f * block_f, axis=1)
    squares = squares.reshape(NC, NYL, 1, micro * toks)

    def rows_of(group):
        return [yl ^ (2 * group + b) for b in range(2)]

    def part(v, group):
        return jnp.stack(
            [lax.dynamic_index_in_dim(v, q, 1, keepdims=False) for q in rows_of(group)]
        ).reshape(1, -1)

    swap = shift(NYH, 1)
    squares = part(squares, yh) + lax.ppermute(part(squares, 1 - yh), "yh", swap)
    place = jnp.stack([(sign * (d - z)) % NX for d in range(NX)])
    kept, sent = gate_parts(
        place, jnp.stack(rows_of(yh) + rows_of(1 - yh)), blocks, weights
    )
    other = lax.ppermute(sent, "yh", swap)
    factor = lax.rsqrt(squares.reshape(-1, 1) / D + norm_eps) * (1.0 / math.sqrt(D))
    gate = (kept + other.astype(jnp.float32)) * factor
    activated = jax.nn.silu(gate).astype(jnp.bfloat16)
    activated = activated.reshape(4, micro, toks, -1).transpose(1, 0, 2, 3)
    return blended, activated.reshape(micro, 4 * toks, -1)


def solution(mesh):
    fine = Mesh(mesh.devices.reshape(SIZES), AXES)
    dp, tensor = ("z", "yl", "c"), ("yh", "x")
    return jax.shard_map(
        body,
        mesh=fine,
        in_specs=(P(dp, tensor, None), P(tensor, dp), P(None, dp, tensor), P(tensor)),
        out_specs=(P(tensor, dp), P(None, tensor, dp)),
        check_vma=False,
    )
```

```python
import math

import jax
import jax.numpy as jnp
from jax import lax
from jax.experimental import pallas as pl
from jax.experimental.pallas import tpu as pltpu
from jax.sharding import Mesh
from jax.sharding import PartitionSpec as P

D = 8192
AXES = ("zh", "zl", "y1", "y0", "c", "yh", "x")
SIZES = (2, 4, 2, 2, 2, 2, 8)
Z, YL, DP, TENSOR = ("zh", "zl"), ("y1", "y0"), ("zh", "zl", "y1", "y0", "c"), ("yh", "x")
NZ, NYL, NX, NZL = 8, 4, 8, 4
LANES = 128

ema_rate = 0.5
norm_eps = 1e-06


def shift(count, by):
    return [(i, (i + by) % count) for i in range(count)]


def spread(v, axes, count):
    return lax.all_to_all(jnp.broadcast_to(v[None], (count,) + v.shape), axes, 0, 0, tiled=True)


def gate_kernel(index, *refs):
    blocks, weights = refs[: 2 * NZ], refs[2 * NZ]
    kept, sent, a_buf, b_buf, acc, a_sem, b_sem = refs[2 * NZ + 1 :]
    b_copies = [
        pltpu.make_async_copy(weights.at[:, q], b_buf.at[q], b_sem.at[q]) for q in range(NZL)
    ]
    a_copies = [
        pltpu.make_async_copy(b, a_buf.at[index[s, 0], index[s, 1], index[s, 2]], a_sem.at[s])
        for s, b in enumerate(blocks)
    ]
    for copy in b_copies + a_copies:
        copy.start()
    for copy in a_copies:
        copy.wait()
    groups, cores, _, rows, depth = a_buf.shape
    cols = b_buf.shape[-1]
    for q in range(NZL):
        b_copies[q].wait()
        left = a_buf[:, :, q].reshape(groups * cores * rows, depth)
        part = jnp.dot(left, b_buf[q].reshape(depth, cols), preferred_element_type=jnp.float32)
        part = part.reshape(groups, cores * rows, cols)
        acc[...] = part if q == 0 else acc[...] + part
    mine = index[2 * NZ, 0]
    kept[...] = acc[mine]
    sent[...] = acc[1 - mine].astype(sent.dtype)


def gate_parts(index, blocks, weights):
    rows, depth = blocks[0].shape
    cols = weights.shape[-1]
    hbm = pl.BlockSpec(memory_space=pl.ANY)
    vmem = pl.BlockSpec(memory_space=pltpu.VMEM)
    return pl.pallas_call(
        gate_kernel,
        out_shape=(
            jax.ShapeDtypeStruct((2 * rows, cols), jnp.float32),
            jax.ShapeDtypeStruct((2 * rows, cols), jnp.bfloat16),
        ),
        in_specs=[pl.BlockSpec(memory_space=pltpu.SMEM)] + [hbm] * (2 * NZ + 1),
        out_specs=(vmem, vmem),
        scratch_shapes=[
            pltpu.VMEM((2, 2, NZL, rows, depth), jnp.bfloat16),
            pltpu.VMEM((NZL, NX, LANES, cols), jnp.bfloat16),
            pltpu.VMEM((2, 2 * rows, cols), jnp.float32),
            pltpu.SemaphoreType.DMA((2 * NZ,)),
            pltpu.SemaphoreType.DMA((NZL,)),
        ],
        compiler_params=pltpu.CompilerParams(vmem_limit_bytes=60 * 2**20),
        cost_estimate=pl.CostEstimate(
            flops=4 * NZ * rows * depth * cols,
            bytes_accessed=2 * NZ * depth * (2 * rows + cols),
            transcendentals=0,
        ),
    )(index, *blocks, weights)


def body(policy, ref_weight, tokens, gain):
    z, c, yh = lax.axis_index(Z), lax.axis_index("c"), lax.axis_index("yh")
    micro, toks, width = tokens.shape
    pieces = tokens.reshape(micro, toks, NZL, LANES).transpose(2, 0, 1, 3)
    pieces = pieces.reshape(NZL * micro, toks, LANES)
    pieces = lax.all_to_all(pieces, ("zl", "y1"), 0, 0, tiled=True)
    pieces = lax.all_to_all(pieces, "x", 0, 0, tiled=True)
    pieces, policy = lax.optimization_barrier((pieces, policy))
    arrived = lax.all_to_all(
        policy.reshape(8, 64, 256).transpose(1, 0, 2), DP, 0, 0, tiled=True
    )
    own = pieces.transpose(1, 0, 2).reshape(toks, NX * LANES)
    own = jnp.concatenate(
        [own] + [lax.ppermute(own, YL, [(i, i ^ e) for i in range(NYL)]) for e in range(1, NYL)]
    )
    rows = own.shape[0]
    own, arrived = lax.optimization_barrier((own, arrived))
    policy_slice = arrived.reshape(ref_weight.shape)
    ref_f = ref_weight.astype(jnp.float32)
    blended = (ref_f + ema_rate * (policy_slice.astype(jnp.float32) - ref_f)).astype(jnp.bfloat16)
    scaled = (blended.astype(jnp.float32) * gain[:, None]).astype(jnp.bfloat16)
    weights = spread(scaled, "x", NX)
    weights = weights.reshape(NX, NZL, LANES, weights.shape[-1])
    blocks, offsets = [own], [0]
    up = down = own
    for step in range(1, NZ // 2 + 1):
        up = lax.ppermute(up, Z, shift(NZ, 1))
        blocks.append(up)
        offsets.append(-step)
        if step < NZ // 2:
            down = lax.ppermute(down, Z, shift(NZ, -1))
            blocks.append(down)
            offsets.append(step)
    others = [lax.ppermute(b, "c", shift(2, 1)) for b in blocks]
    places = [(z + o) % NZ for o in offsets]
    sums = []
    for group in (yh, 1 - yh):
        pair = []
        for held in (blocks, others):
            total = 0.0
            for place, block in zip(places, held):
                block_f = block.astype(jnp.float32)
                part = jnp.sum(block_f * block_f, axis=1)
                total = total + jnp.where(place // NZL == group, part, 0.0)
            pair.append(total[None])
        first, second = pair
        sums.append(
            jnp.concatenate(
                [jnp.where(c == 0, first, second), jnp.where(c == 0, second, first)], axis=1
            )
        )
    swap = shift(2, 1)
    squares = sums[0] + lax.ppermute(sums[1], "yh", swap)
    index = [jnp.stack([p // NZL, core, p % NZL]) for core in (c, 1 - c) for p in places]
    index = jnp.stack(index + [jnp.stack([yh, yh, yh])]).astype(jnp.int32)
    kept, sent = gate_parts(index, blocks + others, weights)
    other = lax.ppermute(sent, "yh", swap)
    factor = lax.rsqrt(squares.reshape(-1, 1) / D + norm_eps) * (1.0 / math.sqrt(D))
    gate = (kept + other.astype(jnp.float32)) * factor
    activated = jax.nn.silu(gate).astype(jnp.bfloat16)
    activated = activated.reshape(2, 2, 2, toks, -1)
    y1, y0 = lax.axis_index("y1"), lax.axis_index("y0")
    activated = jnp.where(y1 == 0, activated, activated[:, ::-1])
    activated = jnp.where(y0 == 0, activated, activated[:, :, ::-1])
    activated = activated.transpose(1, 2, 0, 3, 4)
    return blended, activated.reshape(micro, 4 * toks, -1)


def solution(mesh):
    fine = Mesh(mesh.devices.reshape(SIZES), AXES)
    return jax.shard_map(
        body,
        mesh=fine,
        in_specs=(P(DP, TENSOR, None), P(TENSOR, DP), P(None, DP, TENSOR), P(TENSOR)),
        out_specs=(P(TENSOR, DP), P(None, TENSOR, DP)),
        check_vma=False,
    )
```

```python
import functools
import math

import jax
import jax.numpy as jnp
from jax import lax
from jax.experimental import pallas as pl
from jax.experimental.pallas import tpu as pltpu
from jax.sharding import Mesh
from jax.sharding import PartitionSpec as P

D = 8192
AXES = ("zh", "zl", "y1", "y0", "c", "yh", "x")
SIZES = (2, 4, 2, 2, 2, 2, 8)
Z, YL, DP, TENSOR = ("zh", "zl"), ("y1", "y0"), ("zh", "zl", "y1", "y0", "c"), ("yh", "x")
NZ, NYL, NX, NZL = 8, 4, 8, 4
LANES = 128
TAIL = 16

ema_rate = 0.5
norm_eps = 1e-06


def shift(count, by):
    return [(i, (i + by) % count) for i in range(count)]


def spread(v, axes, count):
    return lax.all_to_all(jnp.broadcast_to(v[None], (count,) + v.shape), axes, 0, 0, tiled=True)


def gate_kernel(first, index, *refs):
    blocks, weights, tail = refs[:NZ], refs[NZ], refs[NZ + 1]
    near, far, extra, a_buf, b_buf, acc, sums, a_sem, b_sem = refs[NZ + (1 if first else 2) :]
    b_copies = [
        pltpu.make_async_copy(weights.at[:, q], b_buf.at[q], b_sem.at[q]) for q in range(NZL)
    ]
    a_copies = [
        pltpu.make_async_copy(b, a_buf.at[index[s, 0], index[s, 1]], a_sem.at[s])
        for s, b in enumerate(blocks)
    ]
    for copy in b_copies + a_copies:
        copy.start()
    for copy in a_copies:
        copy.wait()
    groups, _, rows, depth = a_buf.shape
    cols = b_buf.shape[-1]
    if first:
        sums[...] = jnp.zeros_like(sums)
    for q in range(NZL):
        b_copies[q].wait()
        left = a_buf[:, q].reshape(groups * rows, depth)
        part = jnp.dot(left, b_buf[q].reshape(depth, cols), preferred_element_type=jnp.float32)
        part = part.reshape(groups, rows, cols)
        acc[...] = part if q == 0 else acc[...] + part
        if first:
            for g in range(groups):
                for lane in range(0, depth, LANES):
                    v = a_buf[g, q, :, lane : lane + LANES].astype(jnp.float32)
                    sums[g, :rows] += v * v
    if first:
        for g in range(groups):
            total = jnp.sum(jnp.transpose(sums[g]), axis=0, keepdims=True)
            high = total.astype(jnp.bfloat16).astype(jnp.float32)
            middle = (total - high).astype(jnp.bfloat16).astype(jnp.float32)
            low = total - high - middle
            row = lax.broadcasted_iota(jnp.int32, (TAIL, cols), 0)
            spread_rows = jnp.where(
                row == 0, high, jnp.where(row == 1, middle, jnp.where(row == 2, low, 0.0))
            )
            extra[g] = spread_rows.astype(extra.dtype)
    else:
        extra[...] = tail[...]
    mine = index[NZ, 0]
    for to, g in ((near, mine), (far, 1 - mine)):
        to[:rows] = acc[g].astype(to.dtype)
        to[rows:] = extra[g]


def gate_parts(index, blocks, weights, tail=None):
    rows, depth = blocks[0].shape
    cols = weights.shape[-1]
    hbm = pl.BlockSpec(memory_space=pl.ANY)
    vmem = pl.BlockSpec(memory_space=pltpu.VMEM)
    first = tail is None
    part = jax.ShapeDtypeStruct((rows + TAIL, cols), jnp.bfloat16)
    return pl.pallas_call(
        functools.partial(gate_kernel, first),
        out_shape=(part, part, jax.ShapeDtypeStruct((2, TAIL, cols), jnp.bfloat16)),
        in_specs=[pl.BlockSpec(memory_space=pltpu.SMEM)]
        + [hbm] * (NZ + 1)
        + ([] if first else [vmem]),
        out_specs=(vmem, vmem, vmem),
        scratch_shapes=[
            pltpu.VMEM((2, NZL, rows, depth), jnp.bfloat16),
            pltpu.VMEM((NZL, NX, LANES, cols), jnp.bfloat16),
            pltpu.VMEM((2, rows, cols), jnp.float32),
            pltpu.VMEM((2, cols, LANES), jnp.float32),
            pltpu.SemaphoreType.DMA((NZ,)),
            pltpu.SemaphoreType.DMA((NZL,)),
        ],
        compiler_params=pltpu.CompilerParams(vmem_limit_bytes=60 * 2**20),
        cost_estimate=pl.CostEstimate(
            flops=2 * NZ * rows * depth * cols,
            bytes_accessed=2 * NZ * depth * (rows + cols),
            transcendentals=0,
        ),
    )(index, *blocks, weights, *([] if first else [tail]))


def body(policy, ref_weight, tokens, gain):
    z, c, yh = lax.axis_index(Z), lax.axis_index("c"), lax.axis_index("yh")
    micro, toks, width = tokens.shape
    pieces = tokens.reshape(micro, toks, NZL, LANES).transpose(2, 0, 1, 3)
    pieces = pieces.reshape(NZL * micro, toks, LANES)
    pieces = lax.all_to_all(pieces, ("zl", "y1"), 0, 0, tiled=True)
    pieces = lax.all_to_all(pieces, "x", 0, 0, tiled=True)
    pieces, policy = lax.optimization_barrier((pieces, policy))
    arrived = lax.all_to_all(
        policy.reshape(8, 64, 256).transpose(1, 0, 2), DP, 0, 0, tiled=True
    )
    own = pieces.transpose(1, 0, 2).reshape(toks, NX * LANES)
    own = jnp.concatenate(
        [own] + [lax.ppermute(own, YL, [(i, i ^ e) for i in range(NYL)]) for e in range(1, NYL)]
    )
    rows = own.shape[0]
    own, arrived = lax.optimization_barrier((own, arrived))
    policy_slice = arrived.reshape(ref_weight.shape)
    ref_f = ref_weight.astype(jnp.float32)
    blended = (ref_f + ema_rate * (policy_slice.astype(jnp.float32) - ref_f)).astype(jnp.bfloat16)
    scaled = (blended.astype(jnp.float32) * gain[:, None]).astype(jnp.bfloat16)
    weights = spread(scaled, "x", NX)
    weights = weights.reshape(NX, NZL, LANES, weights.shape[-1])
    blocks, offsets = [own], [0]
    up = down = own
    for step in range(1, NZ // 2 + 1):
        if step > 1:
            up, down = lax.optimization_barrier((up, down))
        up = lax.ppermute(up, Z, shift(NZ, 1))
        blocks.append(up)
        offsets.append(-step)
        if step < NZ // 2:
            down = lax.ppermute(down, Z, shift(NZ, -1))
            blocks.append(down)
            offsets.append(step)
    weights, *blocks[-2:] = lax.optimization_barrier((weights, *blocks[-2:]))
    others = lax.ppermute(weights, "c", shift(2, 1))
    places = [(z + o) % NZ for o in offsets]
    index = [jnp.stack([p // NZL, p % NZL]) for p in places] + [jnp.stack([yh, yh])]
    index = jnp.stack(index).astype(jnp.int32)
    near, far, tail = gate_parts(index, blocks, weights)
    mine = near, lax.ppermute(far, "yh", shift(2, 1))
    near, far, _ = gate_parts(index, blocks, others, tail)
    across = lax.ppermute(far, ("c", "yh"), [(i, 3 - i) for i in range(4)])
    theirs = lax.ppermute(near, "c", shift(2, 1)), across

    def finish(pair):
        total = pair[0].astype(jnp.float32) + pair[1].astype(jnp.float32)
        squares = jnp.sum(total[rows : rows + 3], axis=0)[:rows]
        factor = lax.rsqrt(squares / D + norm_eps) * (1.0 / math.sqrt(D))
        return jax.nn.silu(total[:rows] * factor[:, None]).astype(jnp.bfloat16)

    mine, theirs = finish(mine), finish(theirs)
    activated = jnp.stack([jnp.where(c == 0, mine, theirs), jnp.where(c == 0, theirs, mine)])
    activated = activated.reshape(2, 2, 2, toks, -1)
    y1, y0 = lax.axis_index("y1"), lax.axis_index("y0")
    activated = jnp.where(y1 == 0, activated, activated[:, ::-1])
    activated = jnp.where(y0 == 0, activated, activated[:, :, ::-1])
    activated = activated.transpose(1, 2, 0, 3, 4)
    return blended, activated.reshape(micro, 4 * toks, -1)


def solution(mesh):
    fine = Mesh(mesh.devices.reshape(SIZES), AXES)
    return jax.shard_map(
        body,
        mesh=fine,
        in_specs=(P(DP, TENSOR, None), P(TENSOR, DP), P(None, DP, TENSOR), P(TENSOR)),
        out_specs=(P(TENSOR, DP), P(None, TENSOR, DP)),
        check_vma=False,
    )
```

```python
import functools
import math

import jax
import jax.numpy as jnp
from jax import lax
from jax.experimental import pallas as pl
from jax.experimental.pallas import tpu as pltpu
from jax.sharding import Mesh
from jax.sharding import PartitionSpec as P

D = 8192
AXES = ("zh", "zl", "y1", "y0", "c", "yh", "x")
SIZES = (2, 4, 2, 2, 2, 2, 8)
Z, YL, DP, TENSOR = ("zh", "zl"), ("y1", "y0"), ("zh", "zl", "y1", "y0", "c"), ("yh", "x")
NZ, NYL, NX, NZL = 8, 4, 8, 4
LANES = 128
TAIL = 16

ema_rate = 0.5
norm_eps = 1e-06


def shift(count, by):
    return [(i, (i + by) % count) for i in range(count)]


def spread(v, axes, count):
    return lax.all_to_all(jnp.broadcast_to(v[None], (count,) + v.shape), axes, 0, 0, tiled=True)


def gate_kernel(step, index, *refs):
    held = refs[: (NZ - 1, 1, NZ)[step]]
    weights, refs = refs[len(held)], refs[len(held) + 1 :]
    base = NZ - 1 if step == 1 else 0
    if step == 0:
        acc, sums, a_buf, b_buf, a_sem, b_sem = refs
    elif step == 1:
        acc_in, sums_in, near, far, extra, a_buf, b_buf, acc, sums, a_sem, b_sem = refs
    else:
        tail, near, far, a_buf, b_buf, acc, a_sem, b_sem = refs
    a_copies = [
        pltpu.make_async_copy(h, a_buf.at[s], a_sem.at[s]) for s, h in enumerate(held)
    ]
    if step == 1:
        last = index[NZ + base]
        b_copies = [pltpu.make_async_copy(weights.at[:, last], b_buf.at[last], b_sem.at[0])]
    else:
        b_copies = [
            pltpu.make_async_copy(weights.at[:, q], b_buf.at[q], b_sem.at[q]) for q in range(NZL)
        ]
    for copy in b_copies + a_copies:
        copy.start()
    if step == 1:
        acc[...] = acc_in[...]
        sums[...] = sums_in[...]
    else:
        acc[...] = jnp.zeros_like(acc)
    if step == 0:
        sums[...] = jnp.zeros_like(sums)
    rows, depth = a_buf.shape[1:]
    cols = b_buf.shape[-1]
    for copy in b_copies:
        copy.wait()
    for s, copy in enumerate(a_copies):
        copy.wait()
        g, q = index[base + s], index[NZ + base + s]
        right = b_buf[q].reshape(depth, cols)
        acc[g] += jnp.dot(a_buf[s], right, preferred_element_type=jnp.float32)
        if step < 2:
            total = jnp.zeros((rows, LANES), jnp.float32)
            for lane in range(0, depth, LANES):
                v = a_buf[s, :, lane : lane + LANES].astype(jnp.float32)
                total += v * v
            sums[g, :rows] += total
    if step == 0:
        return
    if step == 1:
        for g in range(2):
            total = jnp.sum(jnp.transpose(sums[g]), axis=0, keepdims=True)
            high = total.astype(jnp.bfloat16).astype(jnp.float32)
            middle = (total - high).astype(jnp.bfloat16).astype(jnp.float32)
            low = total - high - middle
            row = lax.broadcasted_iota(jnp.int32, (TAIL, cols), 0)
            spread_rows = jnp.where(
                row == 0, high, jnp.where(row == 1, middle, jnp.where(row == 2, low, 0.0))
            )
            extra[g] = spread_rows.astype(extra.dtype)
        tail = extra
    mine = index[2 * NZ]
    for to, g in ((near, mine), (far, 1 - mine)):
        to[:rows] = acc[g].astype(to.dtype)
        to[rows:] = tail[g]


def gate_parts(step, index, blocks, weights, *more):
    rows, depth = blocks[0].shape
    cols = weights.shape[-1]
    hbm = pl.BlockSpec(memory_space=pl.ANY)
    vmem = pl.BlockSpec(memory_space=pltpu.VMEM)
    part = jax.ShapeDtypeStruct((rows + TAIL, cols), jnp.bfloat16)
    tail = jax.ShapeDtypeStruct((2, TAIL, cols), jnp.bfloat16)
    acc, sums = (2, rows, cols), (2, cols, LANES)
    totals = [pltpu.VMEM(acc, jnp.float32), pltpu.VMEM(sums, jnp.float32)]
    outs = (
        (jax.ShapeDtypeStruct(acc, jnp.float32), jax.ShapeDtypeStruct(sums, jnp.float32)),
        (part, part, tail),
        (part, part),
    )[step]
    return pl.pallas_call(
        functools.partial(gate_kernel, step),
        out_shape=outs,
        in_specs=[pl.BlockSpec(memory_space=pltpu.SMEM)]
        + [hbm] * (len(blocks) + 1)
        + [vmem] * len(more),
        out_specs=(vmem,) * len(outs),
        scratch_shapes=[
            pltpu.VMEM((len(blocks), rows, depth), jnp.bfloat16),
            pltpu.VMEM((NZL, NX, LANES, cols), jnp.bfloat16),
        ]
        + ([], totals, totals[:1])[step]
        + [pltpu.SemaphoreType.DMA((len(blocks),)), pltpu.SemaphoreType.DMA((NZL,))],
        compiler_params=pltpu.CompilerParams(vmem_limit_bytes=60 * 2**20),
        cost_estimate=pl.CostEstimate(
            flops=2 * len(blocks) * rows * depth * cols,
            bytes_accessed=2 * len(blocks) * depth * (rows + cols),
            transcendentals=0,
        ),
    )(index, *blocks, weights, *more)


def finish_kernel(index, near, far, near_other, far_other, out):
    rows = near.shape[0] - TAIL
    toks = rows // NYL
    core, place = index[2 * NZ + 1], index[2 * NZ + 2]
    for first, second, col in ((near, far, core), (near_other, far_other, 1 - core)):
        squares = first[rows:].astype(jnp.float32) + second[rows:].astype(jnp.float32)
        squares = jnp.sum(squares, axis=0, keepdims=True)
        factor = lax.rsqrt(squares / D + norm_eps) * (1.0 / math.sqrt(D))
        factor = jnp.transpose(jnp.broadcast_to(factor, (LANES, factor.shape[1])))
        for e in range(NYL):
            y = place ^ e
            to = pl.multiple_of(((y % 2) * 2 + col) * toks, 16)
            for lane in range(0, out.shape[2], LANES):
                at = slice(e * toks, (e + 1) * toks), slice(lane, lane + LANES)
                gate = first[at].astype(jnp.float32) + second[at].astype(jnp.float32)
                gate = gate * factor[e * toks : (e + 1) * toks]
                gate = gate / (1.0 + jnp.exp(-gate))
                out[y // 2, pl.ds(to, toks), lane : lane + LANES] = gate.astype(out.dtype)


def finish(index, parts, micro):
    rows, cols = parts[0].shape
    vmem = pl.BlockSpec(memory_space=pltpu.VMEM)
    return pl.pallas_call(
        finish_kernel,
        out_shape=jax.ShapeDtypeStruct((micro, rows - TAIL, cols), jnp.bfloat16),
        in_specs=[pl.BlockSpec(memory_space=pltpu.SMEM)] + [vmem] * 4,
        out_specs=vmem,
        compiler_params=pltpu.CompilerParams(vmem_limit_bytes=8 * 2**20),
    )(index, *parts)


def body(policy, ref_weight, tokens, gain):
    z, c, yh = lax.axis_index(Z), lax.axis_index("c"), lax.axis_index("yh")
    micro, toks, width = tokens.shape
    pieces = tokens.reshape(micro, toks, NZL, LANES).transpose(2, 0, 1, 3)
    pieces = pieces.reshape(NZL * micro, toks, LANES)
    pieces = lax.all_to_all(pieces, ("zl", "y1"), 0, 0, tiled=True)
    pieces = lax.all_to_all(pieces, "x", 0, 0, tiled=True)
    pieces, policy = lax.optimization_barrier((pieces, policy))
    arrived = lax.all_to_all(
        policy.reshape(8, 64, 256).transpose(1, 0, 2), DP, 0, 0, tiled=True
    )
    own = pieces.transpose(1, 0, 2).reshape(toks, NX * LANES)
    own = jnp.concatenate(
        [own] + [lax.ppermute(own, YL, [(i, i ^ e) for i in range(NYL)]) for e in range(1, NYL)]
    )
    rows = own.shape[0]
    own, arrived = lax.optimization_barrier((own, arrived))
    policy_slice = arrived.reshape(ref_weight.shape)
    ref_f = ref_weight.astype(jnp.float32)
    blended = (ref_f + ema_rate * (policy_slice.astype(jnp.float32) - ref_f)).astype(jnp.bfloat16)
    scaled = (blended.astype(jnp.float32) * gain[:, None]).astype(jnp.bfloat16)
    weights = spread(scaled, "x", NX)
    weights = weights.reshape(NX, NZL, LANES, weights.shape[-1])
    blocks, offsets = [own], [0]
    up = down = own
    for step in range(1, NZ // 2 + 1):
        if step > 1:
            up, down = lax.optimization_barrier((up, down))
        up = lax.ppermute(up, Z, shift(NZ, 1))
        blocks.append(up)
        offsets.append(-step)
        if step < NZ // 2:
            down = lax.ppermute(down, Z, shift(NZ, -1))
            blocks.append(down)
            offsets.append(step)
    place = lax.axis_index(YL)
    places = (z + jnp.array(offsets, jnp.int32)) & (NZ - 1)
    index = jnp.concatenate([places // NZL, places % NZL, jnp.stack([yh, c, place])])
    weights, *blocks[-3:-1] = lax.optimization_barrier((weights, *blocks[-3:-1]))
    others = lax.ppermute(weights, "c", shift(2, 1))
    acc, sums = gate_parts(0, index, blocks[:-1], weights)
    acc, blocks[-1] = lax.optimization_barrier((acc, blocks[-1]))
    near, far, tail = gate_parts(1, index, blocks[-1:], weights, acc, sums)
    far = lax.ppermute(far, "yh", shift(2, 1))
    near_other, far_other = gate_parts(2, index, blocks, others, tail)
    far_other = lax.ppermute(far_other, ("c", "yh"), [(i, 3 - i) for i in range(4)])
    near_other = lax.ppermute(near_other, "c", shift(2, 1))
    activated = finish(index, (near, far, near_other, far_other), micro)
    return blended, activated


def solution(mesh):
    fine = Mesh(mesh.devices.reshape(SIZES), AXES)
    return jax.shard_map(
        body,
        mesh=fine,
        in_specs=(P(DP, TENSOR, None), P(TENSOR, DP), P(None, DP, TENSOR), P(TENSOR)),
        out_specs=(P(TENSOR, DP), P(None, TENSOR, DP)),
        check_vma=False,
    )
```

```python
import functools
import math

import jax
import jax.numpy as jnp
from jax import lax
from jax.experimental import pallas as pl
from jax.experimental.pallas import tpu as pltpu
from jax.sharding import Mesh
from jax.sharding import PartitionSpec as P

D = 8192
AXES = ("zh", "zl", "y1", "y0", "c", "yh", "x")
SIZES = (2, 4, 2, 2, 2, 2, 8)
Z, YL, DP, TENSOR = ("zh", "zl"), ("y1", "y0"), ("zh", "zl", "y1", "y0", "c"), ("yh", "x")
NZ, NYL, NX, NZL = 8, 4, 8, 4
LANES = 128
TAIL = 16

ema_rate = 0.5
norm_eps = 1e-06


def shift(count, by):
    return [(i, (i + by) % count) for i in range(count)]


def spread(v, axes, count):
    return lax.all_to_all(jnp.broadcast_to(v[None], (count,) + v.shape), axes, 0, 0, tiled=True)


def gate_kernel(first, index, *refs):
    blocks, weights, refs = refs[: NZ + 1], refs[NZ + 1], refs[NZ + 2 :]
    if first:
        parts, a_buf, b_buf, acc, sums, a_sem, b_sem = refs
    else:
        before, out, a_buf, b_buf, acc, a_sem, b_sem = refs
    groups, _, rows, depth = a_buf.shape
    cols = b_buf.shape[-1]
    b_copies = [
        pltpu.make_async_copy(weights.at[:, q], b_buf.at[q], b_sem.at[q]) for q in range(NZL)
    ]
    places = [a_buf.at[index[s], index[NZ + s]] for s in range(NZ)]
    places[-1:] = [places[-1].at[: rows // 2], places[-1].at[rows // 2 :]]
    a_copies = [
        pltpu.make_async_copy(h, to, a_sem.at[s]) for s, (h, to) in enumerate(zip(blocks, places))
    ]
    for copy in a_copies + b_copies:
        copy.start()
    if first:
        sums[...] = jnp.zeros_like(sums)
    for copy in a_copies:
        copy.wait()
    for q in range(NZL):
        b_copies[q].wait()
        left = a_buf[:, q].reshape(groups * rows, depth)
        part = jnp.dot(left, b_buf[q].reshape(depth, cols), preferred_element_type=jnp.float32)
        part = part.reshape(groups, rows, cols)
        acc[...] = part if q == 0 else acc[...] + part
        if first:
            for g in range(groups):
                total = jnp.zeros((rows, LANES), jnp.float32)
                for lane in range(0, depth, LANES):
                    v = a_buf[g, q, :, lane : lane + LANES].astype(jnp.float32)
                    total += v * v
                sums[g, :rows] += total
    if first:
        for g in range(groups):
            total = jnp.sum(jnp.transpose(sums[g]), axis=0, keepdims=True)
            high = total.astype(jnp.bfloat16).astype(jnp.float32)
            middle = (total - high).astype(jnp.bfloat16).astype(jnp.float32)
            low = total - high - middle
            row = lax.broadcasted_iota(jnp.int32, (TAIL, cols), 0)
            spread_rows = jnp.where(
                row == 0, high, jnp.where(row == 1, middle, jnp.where(row == 2, low, 0.0))
            )
            parts[g, :rows] = acc[g].astype(parts.dtype)
            parts[g, rows:] = spread_rows.astype(parts.dtype)
    else:
        core = index[2 * NZ]
        out[core] = before[...]
        for g in range(groups):
            out[1 - core, g, :rows] = acc[g].astype(out.dtype)
            out[1 - core, g, rows:] = before[g, rows:]


def gate_parts(index, blocks, weights, *before):
    rows, depth = blocks[0].shape
    cols = weights.shape[-1]
    hbm = pl.BlockSpec(memory_space=pl.ANY)
    vmem = pl.BlockSpec(memory_space=pltpu.VMEM)
    first = not before
    parts = (2, rows + TAIL, cols)
    totals = [pltpu.VMEM((2, rows, cols), jnp.float32), pltpu.VMEM((2, cols, LANES), jnp.float32)]
    return pl.pallas_call(
        functools.partial(gate_kernel, first),
        out_shape=jax.ShapeDtypeStruct(parts if first else (2,) + parts, jnp.bfloat16),
        in_specs=[pl.BlockSpec(memory_space=pltpu.SMEM)]
        + [hbm] * (len(blocks) + 1)
        + [vmem] * len(before),
        out_specs=vmem,
        scratch_shapes=[
            pltpu.VMEM((2, NZL, rows, depth), jnp.bfloat16),
            pltpu.VMEM((NZL, NX, LANES, cols), jnp.bfloat16),
        ]
        + (totals if first else totals[:1])
        + [pltpu.SemaphoreType.DMA((len(blocks),)), pltpu.SemaphoreType.DMA((NZL,))],
        compiler_params=pltpu.CompilerParams(vmem_limit_bytes=60 * 2**20),
        cost_estimate=pl.CostEstimate(
            flops=2 * NZ * rows * depth * cols,
            bytes_accessed=2 * NZ * depth * (rows + cols),
            transcendentals=0,
        ),
    )(index, *blocks, weights, *before)


def finish_kernel(index, parts, out):
    rows = parts.shape[1] - TAIL
    toks = rows // NYL
    place = index[2 * NZ + 1]
    for core in range(2):
        a, b = 2 * core, 2 * core + 1
        squares = parts[a, rows:].astype(jnp.float32) + parts[b, rows:].astype(jnp.float32)
        squares = jnp.sum(squares, axis=0, keepdims=True)
        factor = lax.rsqrt(squares / D + norm_eps) * (1.0 / math.sqrt(D))
        factor = jnp.transpose(jnp.broadcast_to(factor, (LANES, factor.shape[1])))
        for e in range(NYL):
            y = place ^ e
            to = pl.multiple_of(((y % 2) * 2 + core) * toks, 16)
            for lane in range(0, out.shape[2], LANES):
                at = slice(e * toks, (e + 1) * toks), slice(lane, lane + LANES)
                gate = parts[(a,) + at].astype(jnp.float32) + parts[(b,) + at].astype(jnp.float32)
                gate = gate * factor[e * toks : (e + 1) * toks]
                gate = gate / (1.0 + jnp.exp(-gate))
                out[y // 2, pl.ds(to, toks), lane : lane + LANES] = gate.astype(out.dtype)


def finish(index, parts, micro):
    _, rows, cols = parts.shape
    vmem = pl.BlockSpec(memory_space=pltpu.VMEM)
    return pl.pallas_call(
        finish_kernel,
        out_shape=jax.ShapeDtypeStruct((micro, rows - TAIL, cols), jnp.bfloat16),
        in_specs=[pl.BlockSpec(memory_space=pltpu.SMEM), vmem],
        out_specs=vmem,
        compiler_params=pltpu.CompilerParams(vmem_limit_bytes=8 * 2**20),
    )(index, parts)


def body(policy, ref_weight, tokens, gain):
    z, c, yh = lax.axis_index(Z), lax.axis_index("c"), lax.axis_index("yh")
    micro, toks, width = tokens.shape
    pieces = tokens.reshape(micro, toks, NZL, LANES).transpose(2, 0, 1, 3)
    pieces = pieces.reshape(NZL * micro, toks, LANES)
    pieces = lax.all_to_all(pieces, ("zl", "y1"), 0, 0, tiled=True)
    pieces = lax.all_to_all(pieces, "x", 0, 0, tiled=True)
    pieces, policy = lax.optimization_barrier((pieces, policy))
    arrived = lax.all_to_all(
        policy.reshape(8, 64, 256).transpose(1, 0, 2), DP, 0, 0, tiled=True
    )
    own = pieces.transpose(1, 0, 2).reshape(toks, NX * LANES)
    own = jnp.concatenate(
        [own] + [lax.ppermute(own, YL, [(i, i ^ e) for i in range(NYL)]) for e in range(1, NYL)]
    )
    rows = own.shape[0]
    own, arrived = lax.optimization_barrier((own, arrived))
    policy_slice = arrived.reshape(ref_weight.shape)
    ref_f = ref_weight.astype(jnp.float32)
    blended = (ref_f + ema_rate * (policy_slice.astype(jnp.float32) - ref_f)).astype(jnp.bfloat16)
    scaled = (blended.astype(jnp.float32) * gain[:, None]).astype(jnp.bfloat16)
    weights = spread(scaled, "x", NX)
    weights = weights.reshape(NX, NZL, LANES, weights.shape[-1])
    blocks, offsets = [own], [0]
    up = down = own
    for step in range(1, NZ // 2):
        if step == NZ // 2 - 1:
            halves = (
                lax.ppermute(up[: rows // 2], Z, shift(NZ, 2)),
                lax.ppermute(down[rows // 2 :], Z, shift(NZ, -2)),
            )
        up = lax.ppermute(up, Z, shift(NZ, 1))
        down = lax.ppermute(down, Z, shift(NZ, -1))
        blocks += [up, down]
        offsets += [-step, step]
    blocks += halves
    offsets.append(NZ // 2)
    places = (z + jnp.array(offsets, jnp.int32)) & (NZ - 1)
    index = jnp.concatenate([places // NZL, places % NZL, jnp.stack([c, lax.axis_index(YL)])])
    weights, index, *blocks[-4:] = lax.optimization_barrier((weights, index, *blocks[-4:]))
    others = lax.ppermute(weights, "c", shift(2, 1))
    parts = gate_parts(index, blocks, weights)
    parts = gate_parts(index, blocks, others, parts)
    parts = lax.all_to_all(parts.reshape(4, *parts.shape[2:]), ("c", "yh"), 0, 0, tiled=True)
    return blended, finish(index, parts, micro)


def solution(mesh):
    fine = Mesh(mesh.devices.reshape(SIZES), AXES)
    return jax.shard_map(
        body,
        mesh=fine,
        in_specs=(P(DP, TENSOR, None), P(TENSOR, DP), P(None, DP, TENSOR), P(TENSOR)),
        out_specs=(P(TENSOR, DP), P(None, TENSOR, DP)),
        check_vma=False,
    )
```

```python
import functools
import math

import jax
import jax.numpy as jnp
from jax import lax
from jax.experimental import pallas as pl
from jax.experimental.pallas import tpu as pltpu
from jax.sharding import Mesh
from jax.sharding import PartitionSpec as P

D = 8192
AXES = ("zh", "zl", "y1", "y0", "c", "yh", "x")
SIZES = (2, 4, 2, 2, 2, 2, 8)
Z, YL, DP, TENSOR = ("zh", "zl"), ("y1", "y0"), ("zh", "zl", "y1", "y0", "c"), ("yh", "x")
NZ, NYL, NX, NZL = 8, 4, 8, 4
LANES = 128
TAIL = 16

ema_rate = 0.5
norm_eps = 1e-06


def shift(count, by):
    return [(i, (i + by) % count) for i in range(count)]


def spread(v, axes, count):
    return lax.all_to_all(jnp.broadcast_to(v[None], (count,) + v.shape), axes, 0, 0, tiled=True)


def gate_kernel(first, index, *refs):
    blocks, weights, refs = refs[: NZ + 1], refs[NZ + 1], refs[NZ + 2 :]
    if first:
        parts, a_buf, b_buf, acc, sums, a_sem, b_sem = refs
    else:
        before, out, a_buf, b_buf, acc, a_sem, b_sem = refs
    groups, _, rows, depth = a_buf.shape
    cols = b_buf.shape[-1]
    x = index[2 * NZ + 2]
    b_copies = [
        pltpu.make_async_copy(weights.at[x ^ e], b_buf.at[:, e], b_sem.at[e]) for e in range(NX)
    ]
    places = [a_buf.at[index[s], index[NZ + s]] for s in range(NZ)]
    places[-1:] = [places[-1].at[: rows // 2], places[-1].at[rows // 2 :]]
    a_copies = [
        pltpu.make_async_copy(h, to, a_sem.at[s]) for s, (h, to) in enumerate(zip(blocks, places))
    ]
    for copy in a_copies + b_copies:
        copy.start()
    if first:
        sums[...] = jnp.zeros_like(sums)
    for copy in a_copies + b_copies:
        copy.wait()
    for q in range(NZL):
        left = a_buf[:, q].reshape(groups * rows, depth)
        part = jnp.dot(left, b_buf[q].reshape(depth, cols), preferred_element_type=jnp.float32)
        part = part.reshape(groups, rows, cols)
        acc[...] = part if q == 0 else acc[...] + part
        if first:
            for g in range(groups):
                total = jnp.zeros((rows, LANES), jnp.float32)
                for lane in range(0, depth, LANES):
                    v = a_buf[g, q, :, lane : lane + LANES].astype(jnp.float32)
                    total += v * v
                sums[g, :rows] += total
    if first:
        for g in range(groups):
            total = jnp.sum(jnp.transpose(sums[g]), axis=0, keepdims=True)
            high = total.astype(jnp.bfloat16).astype(jnp.float32)
            middle = (total - high).astype(jnp.bfloat16).astype(jnp.float32)
            low = total - high - middle
            row = lax.broadcasted_iota(jnp.int32, (TAIL, cols), 0)
            spread_rows = jnp.where(
                row == 0, high, jnp.where(row == 1, middle, jnp.where(row == 2, low, 0.0))
            )
            parts[g, :rows] = acc[g].astype(parts.dtype)
            parts[g, rows:] = spread_rows.astype(parts.dtype)
    else:
        core = index[2 * NZ]
        out[core] = before[...]
        for g in range(groups):
            out[1 - core, g, :rows] = acc[g].astype(out.dtype)
            out[1 - core, g, rows:] = before[g, rows:]


def gate_parts(index, blocks, weights, *before):
    rows, depth = blocks[0].shape
    cols = weights.shape[-1]
    hbm = pl.BlockSpec(memory_space=pl.ANY)
    vmem = pl.BlockSpec(memory_space=pltpu.VMEM)
    first = not before
    parts = (2, rows + TAIL, cols)
    totals = [pltpu.VMEM((2, rows, cols), jnp.float32), pltpu.VMEM((2, cols, LANES), jnp.float32)]
    return pl.pallas_call(
        functools.partial(gate_kernel, first),
        out_shape=jax.ShapeDtypeStruct(parts if first else (2,) + parts, jnp.bfloat16),
        in_specs=[pl.BlockSpec(memory_space=pltpu.SMEM)]
        + [hbm] * (len(blocks) + 1)
        + [vmem] * len(before),
        out_specs=vmem,
        scratch_shapes=[
            pltpu.VMEM((2, NZL, rows, depth), jnp.bfloat16),
            pltpu.VMEM((NZL, NX, LANES, cols), jnp.bfloat16),
        ]
        + (totals if first else totals[:1])
        + [pltpu.SemaphoreType.DMA((len(blocks),)), pltpu.SemaphoreType.DMA((NX,))],
        compiler_params=pltpu.CompilerParams(vmem_limit_bytes=60 * 2**20),
        cost_estimate=pl.CostEstimate(
            flops=2 * NZ * rows * depth * cols,
            bytes_accessed=2 * NZ * depth * (rows + cols),
            transcendentals=0,
        ),
    )(index, *blocks, weights, *before)


def finish_kernel(index, parts, out):
    rows = parts.shape[1] - TAIL
    toks = rows // NYL
    place = index[2 * NZ + 1]
    for core in range(2):
        a, b = 2 * core, 2 * core + 1
        squares = parts[a, rows:].astype(jnp.float32) + parts[b, rows:].astype(jnp.float32)
        squares = jnp.sum(squares, axis=0, keepdims=True)
        factor = lax.rsqrt(squares / D + norm_eps) * (1.0 / math.sqrt(D))
        factor = jnp.transpose(jnp.broadcast_to(factor, (LANES, factor.shape[1])))
        for e in range(NYL):
            y = place ^ e
            to = pl.multiple_of(((y % 2) * 2 + core) * toks, 16)
            for lane in range(0, out.shape[2], LANES):
                at = slice(e * toks, (e + 1) * toks), slice(lane, lane + LANES)
                gate = parts[(a,) + at].astype(jnp.float32) + parts[(b,) + at].astype(jnp.float32)
                gate = gate * factor[e * toks : (e + 1) * toks]
                gate = gate / (1.0 + jnp.exp(-gate))
                out[y // 2, pl.ds(to, toks), lane : lane + LANES] = gate.astype(out.dtype)


def finish(index, parts, micro):
    _, rows, cols = parts.shape
    vmem = pl.BlockSpec(memory_space=pltpu.VMEM)
    return pl.pallas_call(
        finish_kernel,
        out_shape=jax.ShapeDtypeStruct((micro, rows - TAIL, cols), jnp.bfloat16),
        in_specs=[pl.BlockSpec(memory_space=pltpu.SMEM), vmem],
        out_specs=vmem,
        compiler_params=pltpu.CompilerParams(vmem_limit_bytes=8 * 2**20),
    )(index, parts)


def body(policy, ref_weight, tokens, gain):
    z, c, x = lax.axis_index(Z), lax.axis_index("c"), lax.axis_index("x")
    micro, toks, width = tokens.shape
    pieces = tokens.reshape(micro, toks, NZL, LANES).transpose(2, 0, 1, 3)
    pieces = pieces.reshape(NZL * micro, toks, LANES)
    pieces = lax.all_to_all(pieces, ("zl", "y1"), 0, 0, tiled=True)
    pieces, policy = lax.optimization_barrier((pieces, policy))
    arrived = lax.all_to_all(
        policy.reshape(8, 64, 256).transpose(1, 0, 2), DP, 0, 0, tiled=True
    )
    own = []
    for e in range(NX):
        piece = lax.dynamic_index_in_dim(pieces, x ^ e, 0, keepdims=False)
        own.append(lax.ppermute(piece, "x", [(i, i ^ e) for i in range(NX)]) if e else piece)
    own = jnp.concatenate(own, axis=1)
    own, arrived = lax.optimization_barrier((own, arrived))
    own = jnp.concatenate(
        [own] + [lax.ppermute(own, YL, [(i, i ^ e) for i in range(NYL)]) for e in range(1, NYL)]
    )
    rows = own.shape[0]
    policy_slice = arrived.reshape(ref_weight.shape)
    ref_f = ref_weight.astype(jnp.float32)
    blended = (ref_f + ema_rate * (policy_slice.astype(jnp.float32) - ref_f)).astype(jnp.bfloat16)
    scaled = (blended.astype(jnp.float32) * gain[:, None]).astype(jnp.bfloat16)
    weights = spread(scaled, "x", NX)
    weights = weights.reshape(NX, NZL, LANES, weights.shape[-1])
    blocks, offsets = [own], [0]
    up = down = own
    for step in range(1, NZ // 2):
        if step == NZ // 2 - 1:
            halves = (
                lax.ppermute(up[: rows // 2], Z, shift(NZ, 2)),
                lax.ppermute(down[rows // 2 :], Z, shift(NZ, -2)),
            )
        up = lax.ppermute(up, Z, shift(NZ, 1))
        down = lax.ppermute(down, Z, shift(NZ, -1))
        blocks += [up, down]
        offsets += [-step, step]
    blocks += halves
    offsets.append(NZ // 2)
    places = (z + jnp.array(offsets, jnp.int32)) & (NZ - 1)
    index = jnp.concatenate([places // NZL, places % NZL, jnp.stack([c, lax.axis_index(YL), x])])
    weights, index, *blocks[-4:] = lax.optimization_barrier((weights, index, *blocks[-4:]))
    others = lax.ppermute(weights, "c", shift(2, 1))
    parts = gate_parts(index, blocks, weights)
    parts = gate_parts(index, blocks, others, parts)
    parts = lax.all_to_all(parts.reshape(4, *parts.shape[2:]), ("c", "yh"), 0, 0, tiled=True)
    return blended, finish(index, parts, micro)


def solution(mesh):
    fine = Mesh(mesh.devices.reshape(SIZES), AXES)
    return jax.shard_map(
        body,
        mesh=fine,
        in_specs=(P(DP, TENSOR, None), P(TENSOR, DP), P(None, DP, TENSOR), P(TENSOR)),
        out_specs=(P(TENSOR, DP), P(None, TENSOR, DP)),
        check_vma=False,
    )
```

```python
import functools
import math

import jax
import jax.numpy as jnp
from jax import lax
from jax.experimental import pallas as pl
from jax.experimental.pallas import tpu as pltpu
from jax.sharding import Mesh
from jax.sharding import PartitionSpec as P

D = 8192
AXES = ("zh", "zl", "y1", "y0", "c", "yh", "x")
SIZES = (2, 4, 2, 2, 2, 2, 8)
Z, YL, DP, TENSOR = ("zh", "zl"), ("y1", "y0"), ("zh", "zl", "y1", "y0", "c"), ("yh", "x")
NZ, NYL, NX, NZL = 8, 4, 8, 4
LANES = 128
TAIL = 16

ema_rate = 0.5
norm_eps = 1e-06


def shift(count, by):
    return [(i, (i + by) % count) for i in range(count)]


def spread(v, axes, count):
    return lax.all_to_all(jnp.broadcast_to(v[None], (count,) + v.shape), axes, 0, 0, tiled=True)


def gate_kernel(first, index, *refs):
    blocks, weights, refs = refs[: NZ + 1], refs[NZ + 1], refs[NZ + 2 :]
    if first:
        parts, a_buf, b_buf, acc, sums, a_sem, b_sem = refs
    else:
        before, out, a_buf, b_buf, acc, a_sem, b_sem = refs
    groups, _, rows, depth = a_buf.shape
    cols = b_buf.shape[-1]
    b_copies = [
        pltpu.make_async_copy(weights.at[i], b_buf.at[:, i], b_sem.at[i]) for i in range(NX)
    ]
    places = [a_buf.at[index[s], index[NZ + s]] for s in range(NZ)]
    places[-1:] = [places[-1].at[: rows // 2], places[-1].at[rows // 2 :]]
    a_copies = [
        pltpu.make_async_copy(h, to, a_sem.at[s]) for s, (h, to) in enumerate(zip(blocks, places))
    ]
    for copy in a_copies + b_copies:
        copy.start()
    if first:
        sums[...] = jnp.zeros_like(sums)
    for copy in a_copies + b_copies:
        copy.wait()
    for q in range(NZL):
        left = a_buf[:, q].reshape(groups * rows, depth)
        part = jnp.dot(left, b_buf[q].reshape(depth, cols), preferred_element_type=jnp.float32)
        part = part.reshape(groups, rows, cols)
        acc[...] = part if q == 0 else acc[...] + part
        if first:
            for g in range(groups):
                total = jnp.zeros((rows, LANES), jnp.float32)
                for lane in range(0, depth, LANES):
                    v = a_buf[g, q, :, lane : lane + LANES].astype(jnp.float32)
                    total += v * v
                sums[g, :rows] += total
    if first:
        for g in range(groups):
            total = jnp.sum(jnp.transpose(sums[g]), axis=0, keepdims=True)
            high = total.astype(jnp.bfloat16).astype(jnp.float32)
            middle = (total - high).astype(jnp.bfloat16).astype(jnp.float32)
            low = total - high - middle
            row = lax.broadcasted_iota(jnp.int32, (TAIL, cols), 0)
            spread_rows = jnp.where(
                row == 0, high, jnp.where(row == 1, middle, jnp.where(row == 2, low, 0.0))
            )
            parts[g, :rows] = acc[g].astype(parts.dtype)
            parts[g, rows:] = spread_rows.astype(parts.dtype)
    else:
        core = index[2 * NZ]
        out[core] = before[...]
        for g in range(groups):
            out[1 - core, g, :rows] = acc[g].astype(out.dtype)
            out[1 - core, g, rows:] = before[g, rows:]


def gate_parts(index, blocks, weights, *before):
    rows, depth = blocks[0].shape
    cols = weights.shape[-1]
    hbm = pl.BlockSpec(memory_space=pl.ANY)
    vmem = pl.BlockSpec(memory_space=pltpu.VMEM)
    first = not before
    parts = (2, rows + TAIL, cols)
    totals = [pltpu.VMEM((2, rows, cols), jnp.float32), pltpu.VMEM((2, cols, LANES), jnp.float32)]
    return pl.pallas_call(
        functools.partial(gate_kernel, first),
        out_shape=jax.ShapeDtypeStruct(parts if first else (2,) + parts, jnp.bfloat16),
        in_specs=[pl.BlockSpec(memory_space=pltpu.SMEM)]
        + [hbm] * (len(blocks) + 1)
        + [vmem] * len(before),
        out_specs=vmem,
        scratch_shapes=[
            pltpu.VMEM((2, NZL, rows, depth), jnp.bfloat16),
            pltpu.VMEM((NZL, NX, LANES, cols), jnp.bfloat16),
        ]
        + (totals if first else totals[:1])
        + [pltpu.SemaphoreType.DMA((len(blocks),)), pltpu.SemaphoreType.DMA((NX,))],
        compiler_params=pltpu.CompilerParams(vmem_limit_bytes=60 * 2**20),
        cost_estimate=pl.CostEstimate(
            flops=2 * NZ * rows * depth * cols,
            bytes_accessed=2 * NZ * depth * (rows + cols),
            transcendentals=0,
        ),
    )(index, *blocks, weights, *before)


def finish_kernel(index, parts, out):
    rows = parts.shape[1] - TAIL
    toks = rows // NYL
    place = index[2 * NZ + 1]
    for core in range(2):
        a, b = 2 * core, 2 * core + 1
        squares = parts[a, rows:].astype(jnp.float32) + parts[b, rows:].astype(jnp.float32)
        squares = jnp.sum(squares, axis=0, keepdims=True)
        factor = lax.rsqrt(squares / D + norm_eps) * (1.0 / math.sqrt(D))
        factor = jnp.transpose(jnp.broadcast_to(factor, (LANES, factor.shape[1])))
        for e in range(NYL):
            y = place ^ e
            to = pl.multiple_of(((y % 2) * 2 + core) * toks, 16)
            for lane in range(0, out.shape[2], LANES):
                at = slice(e * toks, (e + 1) * toks), slice(lane, lane + LANES)
                gate = parts[(a,) + at].astype(jnp.float32) + parts[(b,) + at].astype(jnp.float32)
                gate = gate * factor[e * toks : (e + 1) * toks]
                gate = gate / (1.0 + jnp.exp(-gate))
                out[y // 2, pl.ds(to, toks), lane : lane + LANES] = gate.astype(out.dtype)


def finish(index, parts, micro):
    _, rows, cols = parts.shape
    vmem = pl.BlockSpec(memory_space=pltpu.VMEM)
    return pl.pallas_call(
        finish_kernel,
        out_shape=jax.ShapeDtypeStruct((micro, rows - TAIL, cols), jnp.bfloat16),
        in_specs=[pl.BlockSpec(memory_space=pltpu.SMEM), vmem],
        out_specs=vmem,
        compiler_params=pltpu.CompilerParams(vmem_limit_bytes=8 * 2**20),
    )(index, parts)


def body(policy, ref_weight, tokens, gain):
    z, c, yh = lax.axis_index(Z), lax.axis_index("c"), lax.axis_index("yh")
    micro, toks, width = tokens.shape
    pieces = tokens.reshape(micro, toks, NZL, LANES).transpose(2, 0, 1, 3)
    pieces = pieces.reshape(NZL * micro, toks, LANES)
    pieces = lax.all_to_all(pieces, ("zl", "y1"), 0, 0, tiled=True)
    pieces = lax.all_to_all(pieces, "x", 0, 0, tiled=True)
    pieces, policy = lax.optimization_barrier((pieces, policy))
    arrived = lax.all_to_all(
        policy.reshape(8, 64, 256).transpose(1, 0, 2), DP, 0, 0, tiled=True
    )
    own = pieces.transpose(1, 0, 2).reshape(toks, NX * LANES)
    for e in (1, 2):
        own = jnp.concatenate([own, lax.ppermute(own, YL, [(i, i ^ e) for i in range(NYL)])])
    rows = own.shape[0]
    own, arrived = lax.optimization_barrier((own, arrived))
    policy_slice = arrived.reshape(ref_weight.shape)
    ref_f = ref_weight.astype(jnp.float32)
    blended = (ref_f + ema_rate * (policy_slice.astype(jnp.float32) - ref_f)).astype(jnp.bfloat16)
    scaled = (blended.astype(jnp.float32) * gain[:, None]).astype(jnp.bfloat16)
    weights = spread(scaled, "x", NX)
    weights = weights.reshape(NX, NZL, LANES, weights.shape[-1])
    blocks, offsets = [own], [0]
    up = down = own
    for step in range(1, NZ // 2):
        if step == NZ // 2 - 1:
            halves = (
                lax.ppermute(up[: rows // 2], Z, shift(NZ, 2)),
                lax.ppermute(down[rows // 2 :], Z, shift(NZ, -2)),
            )
        up = lax.ppermute(up, Z, shift(NZ, 1))
        down = lax.ppermute(down, Z, shift(NZ, -1))
        blocks += [up, down]
        offsets += [-step, step]
    blocks += halves
    offsets.append(NZ // 2)
    places = (z + jnp.array(offsets, jnp.int32)) & (NZ - 1)
    index = jnp.concatenate([places // NZL, places % NZL, jnp.stack([c, lax.axis_index(YL)])])
    weights, index, *blocks[-4:] = lax.optimization_barrier((weights, index, *blocks[-4:]))
    others = lax.ppermute(weights, "c", shift(2, 1))
    parts = gate_parts(index, blocks, weights)
    parts = gate_parts(index, blocks, others, parts)
    parts = lax.all_to_all(parts.reshape(4, *parts.shape[2:]), ("c", "yh"), 0, 0, tiled=True)
    return blended, finish(index, parts, micro)


def solution(mesh):
    fine = Mesh(mesh.devices.reshape(SIZES), AXES)
    return jax.shard_map(
        body,
        mesh=fine,
        in_specs=(P(DP, TENSOR, None), P(TENSOR, DP), P(None, DP, TENSOR), P(TENSOR)),
        out_specs=(P(TENSOR, DP), P(None, TENSOR, DP)),
        check_vma=False,
    )
```

```python
import functools
import math

import jax
import jax.numpy as jnp
from jax import lax
from jax.experimental import pallas as pl
from jax.experimental.pallas import tpu as pltpu
from jax.sharding import Mesh
from jax.sharding import PartitionSpec as P

D = 8192
AXES = ("zh", "zl", "y1", "y0", "c", "yh", "x")
SIZES = (2, 4, 2, 2, 2, 2, 8)
Z, YL, DP, TENSOR = ("zh", "zl"), ("y1", "y0"), ("zh", "zl", "y1", "y0", "c"), ("yh", "x")
NZ, NYL, NX, NZL = 8, 4, 8, 4
LANES = 128
TAIL = 16

ema_rate = 0.5
norm_eps = 1e-06


def shift(count, by):
    return [(i, (i + by) % count) for i in range(count)]


def apart():
    return [
        (z * 2 + c, (z + (2 if c == 0 else -2)) % NZ * 2 + c) for z in range(NZ) for c in range(2)
    ]


def spread(v, axes, count):
    return lax.all_to_all(jnp.broadcast_to(v[None], (count,) + v.shape), axes, 0, 0, tiled=True)


def gate_kernel(first, index, *refs):
    blocks, weights, refs = refs[:NZ], refs[NZ], refs[NZ + 1 :]
    if first:
        parts, a_buf, b_buf, acc, sums, a_sem, b_sem = refs
    else:
        before, out, a_buf, b_buf, acc, a_sem, b_sem = refs
    groups, _, rows, depth = a_buf.shape
    cols = b_buf.shape[-1]
    b_copies = [
        pltpu.make_async_copy(weights.at[i], b_buf.at[:, i], b_sem.at[i]) for i in range(NX)
    ]
    places = [a_buf.at[index[s], index[NZ + s]] for s in range(NZ)]
    a_copies = [
        pltpu.make_async_copy(h, to, a_sem.at[s]) for s, (h, to) in enumerate(zip(blocks, places))
    ]
    for copy in a_copies + b_copies:
        copy.start()
    if first:
        sums[...] = jnp.zeros_like(sums)
    for copy in a_copies + b_copies:
        copy.wait()
    for q in range(NZL):
        left = a_buf[:, q].reshape(groups * rows, depth)
        part = jnp.dot(left, b_buf[q].reshape(depth, cols), preferred_element_type=jnp.float32)
        part = part.reshape(groups, rows, cols)
        acc[...] = part if q == 0 else acc[...] + part
        if first:
            for g in range(groups):
                total = jnp.zeros((rows, LANES), jnp.float32)
                for lane in range(0, depth, LANES):
                    v = a_buf[g, q, :, lane : lane + LANES].astype(jnp.float32)
                    total += v * v
                sums[g, :rows] += total
    if first:
        for g in range(groups):
            total = jnp.sum(jnp.transpose(sums[g]), axis=0, keepdims=True)
            high = total.astype(jnp.bfloat16).astype(jnp.float32)
            middle = (total - high).astype(jnp.bfloat16).astype(jnp.float32)
            low = total - high - middle
            row = lax.broadcasted_iota(jnp.int32, (TAIL, cols), 0)
            spread_rows = jnp.where(
                row == 0, high, jnp.where(row == 1, middle, jnp.where(row == 2, low, 0.0))
            )
            parts[g, :rows] = acc[g].astype(parts.dtype)
            parts[g, rows:] = spread_rows.astype(parts.dtype)
    else:
        core = index[2 * NZ]
        out[core] = before[...]
        for g in range(groups):
            out[1 - core, g, :rows] = acc[g].astype(out.dtype)
            out[1 - core, g, rows:] = before[g, rows:]


def gate_parts(index, blocks, weights, *before):
    rows, depth = blocks[0].shape
    cols = weights.shape[-1]
    hbm = pl.BlockSpec(memory_space=pl.ANY)
    vmem = pl.BlockSpec(memory_space=pltpu.VMEM)
    first = not before
    parts = (2, rows + TAIL, cols)
    totals = [pltpu.VMEM((2, rows, cols), jnp.float32), pltpu.VMEM((2, cols, LANES), jnp.float32)]
    return pl.pallas_call(
        functools.partial(gate_kernel, first),
        out_shape=jax.ShapeDtypeStruct(parts if first else (2,) + parts, jnp.bfloat16),
        in_specs=[pl.BlockSpec(memory_space=pltpu.SMEM)]
        + [hbm] * (len(blocks) + 1)
        + [vmem] * len(before),
        out_specs=vmem,
        scratch_shapes=[
            pltpu.VMEM((2, NZL, rows, depth), jnp.bfloat16),
            pltpu.VMEM((NZL, NX, LANES, cols), jnp.bfloat16),
        ]
        + (totals if first else totals[:1])
        + [pltpu.SemaphoreType.DMA((len(blocks),)), pltpu.SemaphoreType.DMA((NX,))],
        compiler_params=pltpu.CompilerParams(vmem_limit_bytes=60 * 2**20),
        cost_estimate=pl.CostEstimate(
            flops=2 * NZ * rows * depth * cols,
            bytes_accessed=2 * NZ * depth * (rows + cols),
            transcendentals=0,
        ),
    )(index, *blocks, weights, *before)


def finish_kernel(index, parts, out):
    rows = parts.shape[1] - TAIL
    toks = rows // NYL
    place = index[2 * NZ + 1]
    for core in range(2):
        a, b = 2 * core, 2 * core + 1
        squares = parts[a, rows:].astype(jnp.float32) + parts[b, rows:].astype(jnp.float32)
        squares = jnp.sum(squares, axis=0, keepdims=True)
        factor = lax.rsqrt(squares / D + norm_eps) * (1.0 / math.sqrt(D))
        factor = jnp.transpose(jnp.broadcast_to(factor, (LANES, factor.shape[1])))
        for e in range(NYL):
            y = place ^ e
            to = pl.multiple_of(((y % 2) * 2 + core) * toks, 16)
            for lane in range(0, out.shape[2], LANES):
                at = slice(e * toks, (e + 1) * toks), slice(lane, lane + LANES)
                gate = parts[(a,) + at].astype(jnp.float32) + parts[(b,) + at].astype(jnp.float32)
                gate = gate * factor[e * toks : (e + 1) * toks]
                gate = gate / (1.0 + jnp.exp(-gate))
                out[y // 2, pl.ds(to, toks), lane : lane + LANES] = gate.astype(out.dtype)


def finish(index, parts, micro):
    _, rows, cols = parts.shape
    vmem = pl.BlockSpec(memory_space=pltpu.VMEM)
    return pl.pallas_call(
        finish_kernel,
        out_shape=jax.ShapeDtypeStruct((micro, rows - TAIL, cols), jnp.bfloat16),
        in_specs=[pl.BlockSpec(memory_space=pltpu.SMEM), vmem],
        out_specs=vmem,
        compiler_params=pltpu.CompilerParams(vmem_limit_bytes=8 * 2**20),
    )(index, parts)


def body(policy, ref_weight, tokens, gain):
    z, c, yh = lax.axis_index(Z), lax.axis_index("c"), lax.axis_index("yh")
    micro, toks, width = tokens.shape
    pieces = tokens.reshape(micro, toks, NZL, LANES).transpose(2, 0, 1, 3)
    pieces = pieces.reshape(NZL * micro, toks, LANES)
    pieces = lax.all_to_all(pieces, ("zl", "y1"), 0, 0, tiled=True)
    pieces = lax.all_to_all(pieces, "x", 0, 0, tiled=True)
    pieces, policy = lax.optimization_barrier((pieces, policy))
    arrived = lax.all_to_all(
        policy.reshape(8, 64, 256).transpose(1, 0, 2), DP, 0, 0, tiled=True
    )
    own = pieces.transpose(1, 0, 2).reshape(toks, NX * LANES)
    own = jnp.concatenate(
        [own] + [lax.ppermute(own, YL, [(i, i ^ e) for i in range(NYL)]) for e in range(1, NYL)]
    )
    rows = own.shape[0]
    own, arrived = lax.optimization_barrier((own, arrived))
    policy_slice = arrived.reshape(ref_weight.shape)
    ref_f = ref_weight.astype(jnp.float32)
    blended = (ref_f + ema_rate * (policy_slice.astype(jnp.float32) - ref_f)).astype(jnp.bfloat16)
    scaled = (blended.astype(jnp.float32) * gain[:, None]).astype(jnp.bfloat16)
    weights = spread(scaled, "x", NX)
    weights = weights.reshape(NX, NZL, LANES, weights.shape[-1])
    blocks, offsets = [own], [0]
    up = down = own
    for step in range(1, NZ // 2):
        if step == NZ // 2 - 1:
            opposite = lax.ppermute(jnp.where(c == 0, up, down), Z + ("c",), apart())
        up = lax.ppermute(up, Z, shift(NZ, 1))
        down = lax.ppermute(down, Z, shift(NZ, -1))
        blocks += [up, down]
        offsets += [-step, step]
    blocks.append(opposite)
    offsets.append(NZ // 2)
    places = (z + jnp.array(offsets, jnp.int32)) & (NZ - 1)
    index = jnp.concatenate([places // NZL, places % NZL, jnp.stack([c, lax.axis_index(YL)])])
    weights, index, *blocks[-3:] = lax.optimization_barrier((weights, index, *blocks[-3:]))
    others = lax.ppermute(weights, "c", shift(2, 1))
    parts = gate_parts(index, blocks, weights)
    parts = gate_parts(index, blocks, others, parts)
    parts = lax.all_to_all(parts.reshape(4, *parts.shape[2:]), ("c", "yh"), 0, 0, tiled=True)
    return blended, finish(index, parts, micro)


def solution(mesh):
    fine = Mesh(mesh.devices.reshape(SIZES), AXES)
    return jax.shard_map(
        body,
        mesh=fine,
        in_specs=(P(DP, TENSOR, None), P(TENSOR, DP), P(None, DP, TENSOR), P(TENSOR)),
        out_specs=(P(TENSOR, DP), P(None, TENSOR, DP)),
        check_vma=False,
    )
```

```python
import functools
import math

import jax
import jax.numpy as jnp
from jax import lax
from jax.experimental import pallas as pl
from jax.experimental.pallas import tpu as pltpu
from jax.sharding import Mesh
from jax.sharding import PartitionSpec as P

D = 8192
AXES = ("zh", "zl", "y1", "y0", "c", "yh", "x")
SIZES = (2, 4, 2, 2, 2, 2, 8)
Z, YL, DP, TENSOR = ("zh", "zl"), ("y1", "y0"), ("zh", "zl", "y1", "y0", "c"), ("yh", "x")
NZ, NYL, NX, NZL = 8, 4, 8, 4
LANES = 128
TAIL = 16

ema_rate = 0.5
norm_eps = 1e-06


def shift(count, by):
    return [(i, (i + by) % count) for i in range(count)]


def spread(v, axes, count):
    return lax.all_to_all(jnp.broadcast_to(v[None], (count,) + v.shape), axes, 0, 0, tiled=True)


def gate_kernel(first, index, *refs):
    blocks, weights, refs = refs[: NZ + 1], refs[NZ + 1], refs[NZ + 2 :]
    if first:
        parts, a_buf, b_buf, acc, sums, a_sem, b_sem = refs
    else:
        before, out, a_buf, b_buf, acc, a_sem, b_sem = refs
    groups, _, rows, depth = a_buf.shape
    cols = b_buf.shape[-1]
    b_copies = [
        pltpu.make_async_copy(weights.at[i], b_buf.at[:, i], b_sem.at[i]) for i in range(NX)
    ]
    places = [a_buf.at[index[s], index[NZ + s]] for s in range(NZ)]
    places[-1:] = [places[-1].at[: rows // 2], places[-1].at[rows // 2 :]]
    a_copies = [
        pltpu.make_async_copy(h, to, a_sem.at[s]) for s, (h, to) in enumerate(zip(blocks, places))
    ]
    for copy in a_copies + b_copies:
        copy.start()
    if first:
        sums[...] = jnp.zeros_like(sums)
    for copy in a_copies + b_copies:
        copy.wait()
    for q in range(NZL):
        left = a_buf[:, q].reshape(groups * rows, depth)
        part = jnp.dot(left, b_buf[q].reshape(depth, cols), preferred_element_type=jnp.float32)
        part = part.reshape(groups, rows, cols)
        acc[...] = part if q == 0 else acc[...] + part
        if first:
            for g in range(groups):
                total = jnp.zeros((rows, LANES), jnp.float32)
                for lane in range(0, depth, LANES):
                    v = a_buf[g, q, :, lane : lane + LANES].astype(jnp.float32)
                    total += v * v
                sums[g, :rows] += total
    if first:
        for g in range(groups):
            total = jnp.sum(jnp.transpose(sums[g]), axis=0, keepdims=True)
            high = total.astype(jnp.bfloat16).astype(jnp.float32)
            middle = (total - high).astype(jnp.bfloat16).astype(jnp.float32)
            low = total - high - middle
            row = lax.broadcasted_iota(jnp.int32, (TAIL, cols), 0)
            spread_rows = jnp.where(
                row == 0, high, jnp.where(row == 1, middle, jnp.where(row == 2, low, 0.0))
            )
            parts[g, :rows] = acc[g].astype(parts.dtype)
            parts[g, rows:] = spread_rows.astype(parts.dtype)
    else:
        core = index[2 * NZ]
        out[core] = before[...]
        for g in range(groups):
            out[1 - core, g, :rows] = acc[g].astype(out.dtype)
            out[1 - core, g, rows:] = before[g, rows:]


def gate_parts(index, blocks, weights, *before):
    rows, depth = blocks[0].shape
    cols = weights.shape[-1]
    hbm = pl.BlockSpec(memory_space=pl.ANY)
    vmem = pl.BlockSpec(memory_space=pltpu.VMEM)
    first = not before
    parts = (2, rows + TAIL, cols)
    totals = [pltpu.VMEM((2, rows, cols), jnp.float32), pltpu.VMEM((2, cols, LANES), jnp.float32)]
    return pl.pallas_call(
        functools.partial(gate_kernel, first),
        out_shape=jax.ShapeDtypeStruct(parts if first else (2,) + parts, jnp.bfloat16),
        in_specs=[pl.BlockSpec(memory_space=pltpu.SMEM)]
        + [hbm] * (len(blocks) + 1)
        + [vmem] * len(before),
        out_specs=vmem,
        scratch_shapes=[
            pltpu.VMEM((2, NZL, rows, depth), jnp.bfloat16),
            pltpu.VMEM((NZL, NX, LANES, cols), jnp.bfloat16),
        ]
        + (totals if first else totals[:1])
        + [pltpu.SemaphoreType.DMA((len(blocks),)), pltpu.SemaphoreType.DMA((NX,))],
        compiler_params=pltpu.CompilerParams(vmem_limit_bytes=60 * 2**20),
        cost_estimate=pl.CostEstimate(
            flops=2 * NZ * rows * depth * cols,
            bytes_accessed=2 * NZ * depth * (rows + cols),
            transcendentals=0,
        ),
    )(index, *blocks, weights, *before)


def finish_kernel(index, parts, out):
    rows = parts.shape[1] - TAIL
    toks = rows // NYL
    place = index[2 * NZ + 1]
    for core in range(2):
        a, b = 2 * core, 2 * core + 1
        squares = parts[a, rows:].astype(jnp.float32) + parts[b, rows:].astype(jnp.float32)
        squares = jnp.sum(squares, axis=0, keepdims=True)
        factor = lax.rsqrt(squares / D + norm_eps) * (1.0 / math.sqrt(D))
        factor = jnp.transpose(jnp.broadcast_to(factor, (LANES, factor.shape[1])))
        for e in range(NYL):
            y = place ^ e
            to = pl.multiple_of(((y % 2) * 2 + core) * toks, 16)
            for lane in range(0, out.shape[2], LANES):
                at = slice(e * toks, (e + 1) * toks), slice(lane, lane + LANES)
                gate = parts[(a,) + at].astype(jnp.float32) + parts[(b,) + at].astype(jnp.float32)
                gate = gate * factor[e * toks : (e + 1) * toks]
                gate = gate / (1.0 + jnp.exp(-gate))
                out[y // 2, pl.ds(to, toks), lane : lane + LANES] = gate.astype(out.dtype)


def finish(index, parts, micro):
    _, rows, cols = parts.shape
    vmem = pl.BlockSpec(memory_space=pltpu.VMEM)
    return pl.pallas_call(
        finish_kernel,
        out_shape=jax.ShapeDtypeStruct((micro, rows - TAIL, cols), jnp.bfloat16),
        in_specs=[pl.BlockSpec(memory_space=pltpu.SMEM), vmem],
        out_specs=vmem,
        compiler_params=pltpu.CompilerParams(vmem_limit_bytes=8 * 2**20),
    )(index, parts)


def body(policy, ref_weight, tokens, gain):
    z, c, yh = lax.axis_index(Z), lax.axis_index("c"), lax.axis_index("yh")
    micro, toks, width = tokens.shape
    pieces = tokens.reshape(micro, toks, NZL, LANES).transpose(2, 0, 1, 3)
    pieces = pieces.reshape(NZL * micro, toks, LANES)
    pieces = lax.all_to_all(pieces, ("zl", "y1"), 0, 0, tiled=True)
    pieces = lax.all_to_all(pieces, "x", 0, 0, tiled=True)
    pieces, policy = lax.optimization_barrier((pieces, policy))
    arrived = lax.all_to_all(
        policy.reshape(8, 64, 256).transpose(1, 0, 2), DP, 0, 0, tiled=True
    )
    own = pieces.transpose(1, 0, 2).reshape(toks, NX * LANES)
    own = jnp.concatenate(
        [own] + [lax.ppermute(own, YL, [(i, i ^ e) for i in range(NYL)]) for e in range(1, NYL)]
    )
    rows = own.shape[0]
    own, arrived = lax.optimization_barrier((own, arrived))
    policy_slice = arrived.reshape(ref_weight.shape)
    ref_f = ref_weight.astype(jnp.float32)
    blended = (ref_f + ema_rate * (policy_slice.astype(jnp.float32) - ref_f)).astype(jnp.bfloat16)
    scaled = (blended.astype(jnp.float32) * gain[:, None]).astype(jnp.bfloat16)
    weights = spread(scaled, "x", NX)
    weights = weights.reshape(NX, NZL, LANES, weights.shape[-1])
    blocks, offsets = [own], [0]
    up = down = own
    for step in range(1, NZ // 2):
        if step == NZ // 2 - 1:
            halves = (
                lax.ppermute(up[: rows // 2], Z, shift(NZ, 2)),
                lax.ppermute(down[rows // 2 :], Z, shift(NZ, -2)),
            )
        up = lax.ppermute(up, Z, shift(NZ, 1))
        down = lax.ppermute(down, Z, shift(NZ, -1))
        blocks += [up, down]
        offsets += [-step, step]
    blocks += halves
    offsets.append(NZ // 2)
    places = (z + jnp.array(offsets, jnp.int32)) & (NZ - 1)
    index = jnp.concatenate([places // NZL, places % NZL, jnp.stack([c, lax.axis_index(YL)])])
    weights, index, *blocks[-4:] = lax.optimization_barrier((weights, index, *blocks[-4:]))
    others = lax.ppermute(weights, "c", shift(2, 1))
    parts = gate_parts(index, blocks, weights)
    parts = gate_parts(index, blocks, others, parts)
    parts = lax.all_to_all(parts.reshape(4, *parts.shape[2:]), ("c", "yh"), 0, 0, tiled=True)
    return blended, finish(index, parts, micro)


def solution(mesh):
    fine = Mesh(mesh.devices.reshape(SIZES), AXES)
    return jax.shard_map(
        body,
        mesh=fine,
        in_specs=(P(DP, TENSOR, None), P(TENSOR, DP), P(None, DP, TENSOR), P(TENSOR)),
        out_specs=(P(TENSOR, DP), P(None, TENSOR, DP)),
        check_vma=False,
    )
```

```python
import functools
import math

import jax
import jax.numpy as jnp
from jax import lax
from jax.experimental import pallas as pl
from jax.experimental.pallas import tpu as pltpu
from jax.sharding import Mesh
from jax.sharding import PartitionSpec as P

D = 8192
AXES = ("zh", "zl", "y1", "y0", "c", "yh", "x")
SIZES = (2, 4, 2, 2, 2, 2, 8)
Z, YL, DP, TENSOR = ("zh", "zl"), ("y1", "y0"), ("zh", "zl", "y1", "y0", "c"), ("yh", "x")
NZ, NYL, NX, NZL = 8, 4, 8, 4
LANES = 128
TAIL = 16

ema_rate = 0.5
norm_eps = 1e-06


def shift(count, by):
    return [(i, (i + by) % count) for i in range(count)]


def spread(v, axes, count):
    return lax.all_to_all(jnp.broadcast_to(v[None], (count,) + v.shape), axes, 0, 0, tiled=True)


def gate_kernel(first, index, *refs):
    blocks, weights, refs = refs[: NZ + 1], refs[NZ + 1], refs[NZ + 2 :]
    if first:
        parts, a_buf, b_buf, acc, sums, a_sem, b_sem = refs
    else:
        before, out, a_buf, b_buf, acc, a_sem, b_sem = refs
    groups, _, rows, depth = a_buf.shape
    cols = b_buf.shape[-1]
    b_copies = [
        pltpu.make_async_copy(weights.at[i], b_buf.at[:, i], b_sem.at[i]) for i in range(NX)
    ]
    places = [a_buf.at[index[s], index[NZ + s]] for s in range(NZ)]
    places[-1:] = [places[-1].at[: rows // 2], places[-1].at[rows // 2 :]]
    a_copies = [
        pltpu.make_async_copy(h, to, a_sem.at[s]) for s, (h, to) in enumerate(zip(blocks, places))
    ]
    for copy in a_copies + b_copies:
        copy.start()
    if first:
        sums[...] = jnp.zeros_like(sums)
    for copy in a_copies + b_copies:
        copy.wait()
    for q in range(NZL):
        left = a_buf[:, q].reshape(groups * rows, depth)
        part = jnp.dot(left, b_buf[q].reshape(depth, cols), preferred_element_type=jnp.float32)
        part = part.reshape(groups, rows, cols)
        acc[...] = part if q == 0 else acc[...] + part
        if first:
            for g in range(groups):
                total = jnp.zeros((rows, LANES), jnp.float32)
                for lane in range(0, depth, LANES):
                    v = a_buf[g, q, :, lane : lane + LANES].astype(jnp.float32)
                    total += v * v
                sums[g, :rows] += total
    if first:
        for g in range(groups):
            total = jnp.sum(jnp.transpose(sums[g]), axis=0, keepdims=True)
            high = total.astype(jnp.bfloat16).astype(jnp.float32)
            middle = (total - high).astype(jnp.bfloat16).astype(jnp.float32)
            low = total - high - middle
            row = lax.broadcasted_iota(jnp.int32, (TAIL, cols), 0)
            spread_rows = jnp.where(
                row == 0, high, jnp.where(row == 1, middle, jnp.where(row == 2, low, 0.0))
            )
            parts[g, :rows] = acc[g].astype(parts.dtype)
            parts[g, rows:] = spread_rows.astype(parts.dtype)
    else:
        core = index[2 * NZ]
        out[core] = before[...]
        for g in range(groups):
            out[1 - core, g, :rows] = acc[g].astype(out.dtype)
            out[1 - core, g, rows:] = before[g, rows:]


def gate_parts(index, blocks, weights, *before):
    rows, depth = blocks[0].shape
    cols = weights.shape[-1]
    hbm = pl.BlockSpec(memory_space=pl.ANY)
    vmem = pl.BlockSpec(memory_space=pltpu.VMEM)
    first = not before
    parts = (2, rows + TAIL, cols)
    totals = [pltpu.VMEM((2, rows, cols), jnp.float32), pltpu.VMEM((2, cols, LANES), jnp.float32)]
    return pl.pallas_call(
        functools.partial(gate_kernel, first),
        out_shape=jax.ShapeDtypeStruct(parts if first else (2,) + parts, jnp.bfloat16),
        in_specs=[pl.BlockSpec(memory_space=pltpu.SMEM)]
        + [hbm] * (len(blocks) + 1)
        + [vmem] * len(before),
        out_specs=vmem,
        scratch_shapes=[
            pltpu.VMEM((2, NZL, rows, depth), jnp.bfloat16),
            pltpu.VMEM((NZL, NX, LANES, cols), jnp.bfloat16),
        ]
        + (totals if first else totals[:1])
        + [pltpu.SemaphoreType.DMA((len(blocks),)), pltpu.SemaphoreType.DMA((NX,))],
        compiler_params=pltpu.CompilerParams(vmem_limit_bytes=60 * 2**20),
        cost_estimate=pl.CostEstimate(
            flops=2 * NZ * rows * depth * cols,
            bytes_accessed=2 * NZ * depth * (rows + cols),
            transcendentals=0,
        ),
    )(index, *blocks, weights, *before)


def finish_kernel(index, parts, out):
    rows = parts.shape[1] - TAIL
    toks = rows // NYL
    place = index[2 * NZ + 1]
    for core in range(2):
        a, b = 2 * core, 2 * core + 1
        squares = parts[a, rows:].astype(jnp.float32) + parts[b, rows:].astype(jnp.float32)
        squares = jnp.sum(squares, axis=0, keepdims=True)
        factor = lax.rsqrt(squares / D + norm_eps) * (1.0 / math.sqrt(D))
        factor = jnp.transpose(jnp.broadcast_to(factor, (LANES, factor.shape[1])))
        for e in range(NYL):
            y = place ^ e
            to = pl.multiple_of(((y % 2) * 2 + core) * toks, 16)
            for lane in range(0, out.shape[2], LANES):
                at = slice(e * toks, (e + 1) * toks), slice(lane, lane + LANES)
                gate = parts[(a,) + at].astype(jnp.float32) + parts[(b,) + at].astype(jnp.float32)
                gate = gate * factor[e * toks : (e + 1) * toks]
                gate = gate / (1.0 + jnp.exp(-gate))
                out[y // 2, pl.ds(to, toks), lane : lane + LANES] = gate.astype(out.dtype)


def finish(index, parts, micro):
    _, rows, cols = parts.shape
    vmem = pl.BlockSpec(memory_space=pltpu.VMEM)
    return pl.pallas_call(
        finish_kernel,
        out_shape=jax.ShapeDtypeStruct((micro, rows - TAIL, cols), jnp.bfloat16),
        in_specs=[pl.BlockSpec(memory_space=pltpu.SMEM), vmem],
        out_specs=vmem,
        compiler_params=pltpu.CompilerParams(vmem_limit_bytes=8 * 2**20),
    )(index, parts)


def body(policy, ref_weight, tokens, gain):
    z, c, yh = lax.axis_index(Z), lax.axis_index("c"), lax.axis_index("yh")
    micro, toks, width = tokens.shape
    pieces = tokens.reshape(micro, toks, NZL, LANES).transpose(2, 0, 1, 3)
    pieces = pieces.reshape(NZL * micro, toks, LANES)
    pieces = lax.all_to_all(pieces, ("zl", "y1"), 0, 0, tiled=True)
    pieces = lax.all_to_all(pieces, "x", 0, 0, tiled=True)
    first = c == 0
    policy = policy.reshape(8, 64, 256).transpose(1, 0, 2).reshape(32, 2, 8, 256)
    kept = lax.dynamic_index_in_dim(policy, c, 1, keepdims=False)
    swapped = lax.dynamic_index_in_dim(policy, 1 - c, 1, keepdims=False)
    swapped = lax.ppermute(swapped, "c", shift(2, 1))
    policy = jnp.stack(
        [jnp.where(first, kept, swapped), jnp.where(first, swapped, kept)], axis=1
    ).reshape(32, 16, 256)
    pieces, policy = lax.optimization_barrier((pieces, policy))
    arrived = lax.all_to_all(policy, Z + YL, 0, 0, tiled=True)
    own = pieces.transpose(1, 0, 2).reshape(toks, NX * LANES)
    own = jnp.concatenate(
        [own] + [lax.ppermute(own, YL, [(i, i ^ e) for i in range(NYL)]) for e in range(1, NYL)]
    )
    rows = own.shape[0]
    own, arrived = lax.optimization_barrier((own, arrived))
    policy_slice = arrived.reshape(ref_weight.shape)
    ref_f = ref_weight.astype(jnp.float32)
    blended = (ref_f + ema_rate * (policy_slice.astype(jnp.float32) - ref_f)).astype(jnp.bfloat16)
    scaled = (blended.astype(jnp.float32) * gain[:, None]).astype(jnp.bfloat16)
    weights = spread(scaled, "x", NX)
    weights = weights.reshape(NX, NZL, LANES, weights.shape[-1])
    blocks, offsets = [own], [0]
    up = down = own
    for step in range(1, NZ // 2):
        if step == NZ // 2 - 1:
            halves = (
                lax.ppermute(up[: rows // 2], Z, shift(NZ, 2)),
                lax.ppermute(down[rows // 2 :], Z, shift(NZ, -2)),
            )
        up = lax.ppermute(up, Z, shift(NZ, 1))
        down = lax.ppermute(down, Z, shift(NZ, -1))
        blocks += [up, down]
        offsets += [-step, step]
    blocks += halves
    offsets.append(NZ // 2)
    places = (z + jnp.array(offsets, jnp.int32)) & (NZ - 1)
    index = jnp.concatenate([places // NZL, places % NZL, jnp.stack([c, lax.axis_index(YL)])])
    weights, index, *blocks[-4:] = lax.optimization_barrier((weights, index, *blocks[-4:]))
    others = lax.ppermute(weights, "c", shift(2, 1))
    parts = gate_parts(index, blocks, weights)
    parts = gate_parts(index, blocks, others, parts)
    parts = lax.all_to_all(parts.reshape(4, *parts.shape[2:]), ("c", "yh"), 0, 0, tiled=True)
    return blended, finish(index, parts, micro)


def solution(mesh):
    fine = Mesh(mesh.devices.reshape(SIZES), AXES)
    return jax.shard_map(
        body,
        mesh=fine,
        in_specs=(P(DP, TENSOR, None), P(TENSOR, DP), P(None, DP, TENSOR), P(TENSOR)),
        out_specs=(P(TENSOR, DP), P(None, TENSOR, DP)),
        check_vma=False,
    )
```

```python
import functools
import math

import jax
import jax.numpy as jnp
from jax import lax
from jax.experimental import pallas as pl
from jax.experimental.pallas import tpu as pltpu
from jax.sharding import Mesh
from jax.sharding import PartitionSpec as P

D = 8192
AXES = ("zh", "zl", "y1", "y0", "c", "yh", "x")
SIZES = (2, 4, 2, 2, 2, 2, 8)
Z, YL, DP, TENSOR = ("zh", "zl"), ("y1", "y0"), ("zh", "zl", "y1", "y0", "c"), ("yh", "x")
NZ, NYL, NX, NZL = 8, 4, 8, 4
LANES = 128
TAIL = 16

ema_rate = 0.5
norm_eps = 1e-06


def shift(count, by):
    return [(i, (i + by) % count) for i in range(count)]


def spread(v, axes, count):
    return lax.all_to_all(jnp.broadcast_to(v[None], (count,) + v.shape), axes, 0, 0, tiled=True)


def gate_kernel(first, index, *refs):
    blocks, weights, refs = refs[: NZ + 1], refs[NZ + 1], refs[NZ + 2 :]
    if first:
        parts, a_buf, b_buf, acc, sums, a_sem, b_sem = refs
    else:
        before, out, a_buf, b_buf, acc, a_sem, b_sem = refs
    groups, _, rows, depth = a_buf.shape
    cols = b_buf.shape[-1]
    b_copies = [
        pltpu.make_async_copy(weights.at[i], b_buf.at[:, i], b_sem.at[i]) for i in range(NX)
    ]
    places = [a_buf.at[index[s], index[NZ + s]] for s in range(NZ)]
    places[-1:] = [places[-1].at[: rows // 2], places[-1].at[rows // 2 :]]
    a_copies = [
        pltpu.make_async_copy(h, to, a_sem.at[s]) for s, (h, to) in enumerate(zip(blocks, places))
    ]
    for copy in a_copies + b_copies:
        copy.start()
    if first:
        sums[...] = jnp.zeros_like(sums)
    for copy in a_copies + b_copies:
        copy.wait()
    for q in range(NZL):
        left = a_buf[:, q].reshape(groups * rows, depth)
        part = jnp.dot(left, b_buf[q].reshape(depth, cols), preferred_element_type=jnp.float32)
        part = part.reshape(groups, rows, cols)
        acc[...] = part if q == 0 else acc[...] + part
        if first:
            for g in range(groups):
                total = jnp.zeros((rows, LANES), jnp.float32)
                for lane in range(0, depth, LANES):
                    v = a_buf[g, q, :, lane : lane + LANES].astype(jnp.float32)
                    total += v * v
                sums[g, :rows] += total
    if first:
        for g in range(groups):
            total = jnp.sum(jnp.transpose(sums[g]), axis=0, keepdims=True)
            high = total.astype(jnp.bfloat16).astype(jnp.float32)
            middle = (total - high).astype(jnp.bfloat16).astype(jnp.float32)
            low = total - high - middle
            row = lax.broadcasted_iota(jnp.int32, (TAIL, cols), 0)
            spread_rows = jnp.where(
                row == 0, high, jnp.where(row == 1, middle, jnp.where(row == 2, low, 0.0))
            )
            parts[g, :rows] = acc[g].astype(parts.dtype)
            parts[g, rows:] = spread_rows.astype(parts.dtype)
    else:
        core = index[2 * NZ]
        out[core] = before[...]
        for g in range(groups):
            out[1 - core, g, :rows] = acc[g].astype(out.dtype)
            out[1 - core, g, rows:] = before[g, rows:]


def gate_parts(index, blocks, weights, *before):
    rows, depth = blocks[0].shape
    cols = weights.shape[-1]
    hbm = pl.BlockSpec(memory_space=pl.ANY)
    vmem = pl.BlockSpec(memory_space=pltpu.VMEM)
    first = not before
    parts = (2, rows + TAIL, cols)
    totals = [pltpu.VMEM((2, rows, cols), jnp.float32), pltpu.VMEM((2, cols, LANES), jnp.float32)]
    return pl.pallas_call(
        functools.partial(gate_kernel, first),
        out_shape=jax.ShapeDtypeStruct(parts if first else (2,) + parts, jnp.bfloat16),
        in_specs=[pl.BlockSpec(memory_space=pltpu.SMEM)]
        + [hbm] * (len(blocks) + 1)
        + [vmem] * len(before),
        out_specs=vmem,
        scratch_shapes=[
            pltpu.VMEM((2, NZL, rows, depth), jnp.bfloat16),
            pltpu.VMEM((NZL, NX, LANES, cols), jnp.bfloat16),
        ]
        + (totals if first else totals[:1])
        + [pltpu.SemaphoreType.DMA((len(blocks),)), pltpu.SemaphoreType.DMA((NX,))],
        compiler_params=pltpu.CompilerParams(vmem_limit_bytes=60 * 2**20),
        cost_estimate=pl.CostEstimate(
            flops=2 * NZ * rows * depth * cols,
            bytes_accessed=2 * NZ * depth * (rows + cols),
            transcendentals=0,
        ),
    )(index, *blocks, weights, *before)


def finish_kernel(index, parts, out):
    rows = parts.shape[1] - TAIL
    toks = rows // NYL
    place = index[2 * NZ + 1]
    for core in range(2):
        a, b = 2 * core, 2 * core + 1
        squares = parts[a, rows:].astype(jnp.float32) + parts[b, rows:].astype(jnp.float32)
        squares = jnp.sum(squares, axis=0, keepdims=True)
        factor = lax.rsqrt(squares / D + norm_eps) * (1.0 / math.sqrt(D))
        factor = jnp.transpose(jnp.broadcast_to(factor, (LANES, factor.shape[1])))
        for e in range(NYL):
            y = place ^ e
            to = pl.multiple_of(((y % 2) * 2 + core) * toks, 16)
            for lane in range(0, out.shape[2], LANES):
                at = slice(e * toks, (e + 1) * toks), slice(lane, lane + LANES)
                gate = parts[(a,) + at].astype(jnp.float32) + parts[(b,) + at].astype(jnp.float32)
                gate = gate * factor[e * toks : (e + 1) * toks]
                gate = gate / (1.0 + jnp.exp(-gate))
                out[y // 2, pl.ds(to, toks), lane : lane + LANES] = gate.astype(out.dtype)


def finish(index, parts, micro):
    _, rows, cols = parts.shape
    vmem = pl.BlockSpec(memory_space=pltpu.VMEM)
    return pl.pallas_call(
        finish_kernel,
        out_shape=jax.ShapeDtypeStruct((micro, rows - TAIL, cols), jnp.bfloat16),
        in_specs=[pl.BlockSpec(memory_space=pltpu.SMEM), vmem],
        out_specs=vmem,
        compiler_params=pltpu.CompilerParams(vmem_limit_bytes=8 * 2**20),
    )(index, parts)


def body(policy, ref_weight, tokens, gain):
    z, c, yh = lax.axis_index(Z), lax.axis_index("c"), lax.axis_index("yh")
    micro, toks, width = tokens.shape
    pieces = tokens.reshape(micro, toks, NZL, LANES).transpose(2, 0, 1, 3)
    pieces = pieces.reshape(NZL * micro, toks, LANES)
    pieces = lax.all_to_all(pieces, ("zl", "y1"), 0, 0, tiled=True)
    pieces = lax.all_to_all(pieces, "x", 0, 0, tiled=True)
    first = c == 0
    policy = policy.reshape(8, 64, 256).transpose(1, 0, 2).reshape(32, 2, 8, 256)
    kept = lax.dynamic_index_in_dim(policy, c, 1, keepdims=False)
    swapped = lax.dynamic_index_in_dim(policy, 1 - c, 1, keepdims=False)
    swapped = lax.ppermute(swapped, "c", shift(2, 1))
    policy = jnp.stack(
        [jnp.where(first, kept, swapped), jnp.where(first, swapped, kept)], axis=1
    ).reshape(32, 16, 256)
    pieces, policy = lax.optimization_barrier((pieces, policy))
    arrived = lax.all_to_all(policy, Z + YL, 0, 0, tiled=True)
    own = pieces.transpose(1, 0, 2).reshape(toks, NX * LANES)
    others = [lax.ppermute(own, YL, [(i, i ^ e) for i in range(NYL)]) for e in range(1, NYL)]
    *others[:2], arrived = lax.optimization_barrier((*others[:2], arrived))
    own = jnp.concatenate([own] + others)
    rows = own.shape[0]
    policy_slice = arrived.reshape(ref_weight.shape)
    ref_f = ref_weight.astype(jnp.float32)
    blended = (ref_f + ema_rate * (policy_slice.astype(jnp.float32) - ref_f)).astype(jnp.bfloat16)
    scaled = (blended.astype(jnp.float32) * gain[:, None]).astype(jnp.bfloat16)
    weights = spread(scaled, "x", NX)
    weights = weights.reshape(NX, NZL, LANES, weights.shape[-1])
    blocks, offsets = [own], [0]
    up = down = own
    for step in range(1, NZ // 2):
        if step == NZ // 2 - 1:
            halves = (
                lax.ppermute(up[: rows // 2], Z, shift(NZ, 2)),
                lax.ppermute(down[rows // 2 :], Z, shift(NZ, -2)),
            )
        up = lax.ppermute(up, Z, shift(NZ, 1))
        down = lax.ppermute(down, Z, shift(NZ, -1))
        blocks += [up, down]
        offsets += [-step, step]
    blocks += halves
    offsets.append(NZ // 2)
    places = (z + jnp.array(offsets, jnp.int32)) & (NZ - 1)
    index = jnp.concatenate([places // NZL, places % NZL, jnp.stack([c, lax.axis_index(YL)])])
    weights, index, *blocks[-4:] = lax.optimization_barrier((weights, index, *blocks[-4:]))
    others = lax.ppermute(weights, "c", shift(2, 1))
    parts = gate_parts(index, blocks, weights)
    parts = gate_parts(index, blocks, others, parts)
    parts = lax.all_to_all(parts.reshape(4, *parts.shape[2:]), ("c", "yh"), 0, 0, tiled=True)
    return blended, finish(index, parts, micro)


def solution(mesh):
    fine = Mesh(mesh.devices.reshape(SIZES), AXES)
    return jax.shard_map(
        body,
        mesh=fine,
        in_specs=(P(DP, TENSOR, None), P(TENSOR, DP), P(None, DP, TENSOR), P(TENSOR)),
        out_specs=(P(TENSOR, DP), P(None, TENSOR, DP)),
        check_vma=False,
    )
```
